32 devices in a mesh: section: 4 (over x, core), seq: 2 (over y), expert: 4 (over z).
Axes of the slice: x: 2, y: 2, z: 4, core: 2. Of those that a mesh axis runs over, the one named last changes fastest.
Arguments:
- queries: bfloat16 [16, 192, 4096], P(('section', 'expert'), 'seq'), may hold values from -112 to 112
- dec_state: bfloat16 [16, 192, 4096], P(('section', 'expert'), 'seq'), may hold values from -6 to 6
- enc_kv: bfloat16 [2, 16, 320, 1024], P(None, ('section', 'expert'), 'seq'), may hold values from -15 to 15
- band_start: int32 [16, 2], P(('section', 'expert'), 'seq'), may hold values from 0 to 192, as said below
- norm_gain: float32 [4096], replicated, may hold values from 0.5 to 1.5
- route_ids: int32 [16, 192, 1], P(('section', 'expert'), 'seq'), may hold values from 0 to 3; in each aligned block of 96 rows (0 to 95, 96 to 191, ..., all dimensions but the last counted through in order) at most 24 rows name the same one
- keep: int32 [16, 192], P(('section', 'expert'), 'seq'), may hold values 0 or 1
- route_prob: float32 [16, 192], P(('section', 'expert'), 'seq'), may hold values from 0.25 to 1
- w_in: bfloat16 [4, 5120, 4096], P('seq', ('section', 'expert')), may hold values from -0.09375 to 0.09375
- w_out: bfloat16 [4, 5120, 4096], P('seq', ('section', 'expert')), may hold values from -0.078125 to 0.078125
Outputs:
- mixed: bfloat16 [16, 192, 4096], P(('section', 'expert'), 'seq')
The draws below stay inside these ranges and needn't reach their ends.
Inputs may be any that keep to these rules, and one draw needn't show every extreme that they name: `band_start`: block q's band lies within encoder frames (q - 1) * 160 to (q + 2) * 160 - 1. `route_ids`: among the tokens of one device no expert is named more than 24 times.
All inputs are finite; a program needn't handle non-finite values. No bound on the sum of `keep` on one device may be relied on, other than what follows from the above.
Results may differ from the reference program's by a relative error of at most 0.011.
Values may be sent and summed in bfloat16 or wider, within the bound.
No kernel may reach another device: no remote copies, remote signals or barrier semaphores. Data moves between devices by JAX's collectives and lax.ppermute only.
A program may use at most 128 MiB of HBM per device.

```python
import math
import jax
import jax.numpy as jnp
import numpy as np
from jax import lax

D = 4096
HEADS = 32
KV_HEADS = 8
DH = 128
FF = 5120
WIN = 128
FR_DEV = 160
TOK_DEV = 96
UTT_SECTION = 4
UTT = 16
FRAMES = 320
TOKENS = 192
EXPERTS = 4
CAP = 24
GROUP = 16
FS = 320
N_SEQ = 2


def band_offsets(key):
    blocks = jnp.arange(N_SEQ, dtype=jnp.int32)[None, :]
    utterances = jnp.arange(UTT, dtype=jnp.int32)[:, None]
    jitter = jax.random.randint(jax.random.fold_in(key, 11), (UTT, N_SEQ), -FR_DEV, 2 * FR_DEV - WIN + 1, dtype=jnp.int32)
    starts = jnp.clip(blocks * FR_DEV + jitter, 0, FRAMES - WIN)
    starts = jnp.where((utterances == 0) & (blocks == 0), 0, starts)
    starts = jnp.where((utterances == UTT - 1) & (blocks == N_SEQ - 1), FRAMES - WIN, starts)
    return starts.astype(jnp.int32)


def key_values(key):
    keys_raw = jax.random.normal(jax.random.fold_in(key, 22), (UTT, FRAMES, KV_HEADS * DH), jnp.float32)
    keys_raw = jnp.clip(keys_raw, -6.0, 6.0)
    values_raw = jnp.clip(2.5 * jax.random.normal(jax.random.fold_in(key, 24), (UTT, FRAMES, KV_HEADS * DH), jnp.float32), -15.0, 15.0)
    return (keys_raw, values_raw)


def draw_band_start(key, part):
    return band_offsets(key)


def draw_enc_kv(key, part):
    keys_raw, values_raw = key_values(key)
    return jnp.stack([keys_raw, values_raw]).astype(jnp.bfloat16)


def draw_queries(key, part):
    drawn = jnp.clip(jax.random.normal(jax.random.fold_in(key, 31), (UTT, TOKENS, D), jnp.float32), -6.0, 6.0)
    return drawn.astype(jnp.bfloat16)


def set_ends(drawn, stream_key, low, top_value):
    spot = [jax.random.randint(jax.random.fold_in(stream_key, axis), (), 0, length) for axis, length in enumerate(drawn.shape)]
    widest = drawn.shape.index(max(drawn.shape))
    neighbour = spot[:widest] + [(spot[widest] + 1) % drawn.shape[widest]] + spot[widest + 1:]
    return drawn.at[tuple(spot)].set(low).at[tuple(neighbour)].set(top_value)


def block_levels(stream_key, extent, cuts, low, largest):
    factor_of, own = 1.0, jax.random.fold_in(stream_key, 6)
    for axis_at, shards_of in cuts:
        draws = jnp.exp(jax.random.uniform(jax.random.fold_in(own, axis_at), (shards_of,), jnp.float32, low / len(cuts), largest / len(cuts)))
        factor_of = factor_of * jnp.repeat(draws, extent[axis_at] // shards_of).reshape([-1 if axis == axis_at else 1 for axis in range(len(extent))])
    return factor_of


def deal_out(stream_key, own, number, rows, count, top, most, slope):
    sequence = jax.random.permutation(stream_key, count)
    packed, common = portions_of(count, rows * top, most, slope, True), portions_of(count, rows * top, most, slope, False)
    places = jnp.arange(count)

    def named(lengths, turn):
        used = int((lengths > 0).sum())
        fixed = max(1, used // 4)
        shifted = fixed + (places - fixed + turn * (used - fixed)) % max(1, count - fixed)
        return jnp.zeros((count,), jnp.int32).at[sequence[jnp.where(places < fixed, places, shifted)]].set(jnp.asarray(lengths, jnp.int32))

    lengths = jnp.where(number % 4 == 0, named(packed, number // 4), named(common, number - number // 4 - 1))
    mixed = jax.random.permutation(jax.random.fold_in(own, 3), count)
    giver, receiver = mixed[0:count // 2 * 2:2], mixed[1:count // 2 * 2:2]
    room = jnp.minimum(lengths[giver] - 1, most - lengths[receiver]) // 2
    room = jnp.where((giver == sequence[0]) | (receiver == sequence[0]) | (lengths[receiver] == 0), 0, jnp.maximum(room, 0))
    shifted = jax.random.randint(jax.random.fold_in(own, 4), (count // 2,), 0, 1 << 20) % (room + 1)
    lengths = lengths.at[giver].add(-shifted).at[receiver].add(shifted)
    items = jnp.searchsorted(jnp.cumsum(lengths), jnp.arange(rows * top), side="right").astype(jnp.int32)
    table = items.reshape(top, rows).T
    table = table[jax.random.permutation(jax.random.fold_in(own, 1), rows)]
    turn = jax.random.randint(jax.random.fold_in(own, 2), (rows, 1), 0, top)
    return jnp.take_along_axis(table, (jnp.arange(top)[None, :] + turn) % top, axis=1)


def portions_of(amount, total, reach, skew, full):
    weights = [(1 << 20) // math.isqrt(standing ** skew) + 1 for standing in range(1, amount + 1)]
    largest = reach if full else min(reach, max(-(-total // amount), total * weights[0] // sum(weights)))
    least = 1 if total - largest >= amount - 1 else 0
    holding, spare = [largest] + [least] * (amount - 1), total - largest - least * (amount - 1)
    while spare > 0:
        free = [i for i in range(1, amount) if holding[i] < largest] or [i for i in range(1, amount) if holding[i] < reach]
        mass, remaining = sum([weights[i] for i in free]), spare
        for i in free:
            addition = min(reach - holding[i], max(1, remaining * weights[i] // mass), spare)
            holding[i] = holding[i] + addition
            spare = spare - addition
    return np.array(holding)


def centred(rng, shape, spread, most, cuts=(), kind=jnp.bfloat16):
    values = spread * jax.random.normal(rng, shape, jnp.float32)
    if cuts:
        values = values * block_levels(rng, shape, cuts, -0.22, 0.18)
    return jnp.clip(values, -most, most).astype(kind)


def setup_inputs(seed: int = 0) -> dict:
    keys = jax.random.split(jax.random.key(seed), 11)
    queries = draw_queries(jax.random.fold_in(keys[10], 71), 0)
    dec_state = centred(keys[1], (UTT, TOKENS, D), 1.0, 6.0, ((0, 16), (1, 2)))
    enc_kv = draw_enc_kv(jax.random.fold_in(keys[10], 71), 0)
    band_start = draw_band_start(jax.random.fold_in(keys[10], 71), 0)
    norm_gain = jnp.clip(1.0 + 0.1 * jax.random.normal(keys[4], (D,), jnp.float32), 0.5, 1.5)
    route_ids_keys = jax.random.split(jax.random.fold_in(keys[5], 1), UTT * TOKENS // TOK_DEV)
    route_ids_turns = jax.random.permutation(jax.random.fold_in(keys[5], 3), UTT * TOKENS // TOK_DEV)
    route_ids = jax.vmap(lambda own, number: deal_out(jax.random.fold_in(keys[5], 2), own, number, TOK_DEV, EXPERTS, 1, CAP, 2))(route_ids_keys, route_ids_turns).reshape((UTT, TOKENS, 1))
    keep = set_ends((jax.random.randint(keys[6], (UTT, TOKENS), 0, 8) < 7).astype(jnp.int32), jax.random.fold_in(keys[6], 1), 0, 1)
    route_prob = jnp.clip(0.25 + 0.75 * jax.random.uniform(keys[7], (UTT, TOKENS), jnp.float32) ** block_levels(keys[7], (UTT, TOKENS), ((0, 16), (1, 2)), -0.2, 0.2), 0.25, 1.0)
    w_in = centred(keys[8], (EXPERTS, FF, D), D ** -0.5, 0.09375, ((0, 2), (1, 16)))
    w_out = centred(keys[9], (EXPERTS, FF, D), FF ** -0.5, 0.078125, ((0, 2), (1, 16)))
    return dict(queries=queries, dec_state=dec_state, enc_kv=enc_kv, band_start=band_start, norm_gain=norm_gain, route_ids=route_ids, keep=keep, route_prob=route_prob, w_in=w_in, w_out=w_out)


def cross_attend(query_rows, band_pair):
    tok_count = query_rows.shape[0]
    groups = HEADS // KV_HEADS
    queries_f = query_rows.astype(jnp.float32).reshape(tok_count, KV_HEADS, groups, DH)
    keys_f = band_pair[0].astype(jnp.float32).reshape(WIN, KV_HEADS, DH)
    values_f = band_pair[1].astype(jnp.float32).reshape(WIN, KV_HEADS, DH)
    scores = jnp.einsum('tkgd,wkd->kgtw', queries_f, keys_f) / math.sqrt(DH)
    row_peak = lax.optimization_barrier(jnp.max(scores, axis=-1, keepdims=True))
    weights = jnp.exp(scores - row_peak)
    row_total = lax.optimization_barrier(jnp.sum(weights, axis=-1))
    rounded = lax.optimization_barrier(weights.astype(jnp.bfloat16)).astype(jnp.float32)
    context = jnp.einsum('kgtw,wkd->tkgd', rounded, values_f) / jnp.transpose(row_total, (2, 0, 1))[..., None]
    return context.reshape(tok_count, HEADS * DH)

def reference(queries, dec_state, enc_kv, band_start, norm_gain, route_ids, keep, route_prob, w_in, w_out):
    producer = jnp.moveaxis(jnp.roll(enc_kv, UTT_SECTION, axis=1), 1, 0)
    query_blocks = queries.reshape(UTT, N_SEQ, TOK_DEV, D)

    def one_block(query_rows, pair, first_frame):
        band_pair = lax.dynamic_slice_in_dim(pair, first_frame.astype(jnp.int32), WIN, 1)
        return cross_attend(query_rows, band_pair)

    def one_utterance(block_rows, pair, firsts):
        return jax.vmap(lambda rows_q, first_frame: one_block(rows_q, pair, first_frame))(block_rows, firsts)
    context = jax.vmap(one_utterance)(query_blocks, producer, band_start).reshape(UTT, TOKENS, D)
    state = dec_state.astype(jnp.float32) + context
    normed = (state * lax.rsqrt(lax.optimization_barrier(jnp.mean(state * state, axis=-1, keepdims=True)) + 1e-06) * norm_gain).astype(jnp.bfloat16)
    flat_rows = normed.reshape(-1, D)
    count_all = flat_rows.shape[0]
    experts_of = route_ids.reshape(-1).astype(jnp.int32)
    row_limit = UTT * N_SEQ * CAP
    order = jnp.argsort(experts_of, stable=True)
    sorted_rows = jnp.concatenate([flat_rows[order], jnp.zeros((row_limit, D), jnp.bfloat16)], axis=0)
    loads = lax.optimization_barrier(jnp.sum((experts_of[None, :] == jnp.arange(EXPERTS, dtype=jnp.int32)[:, None]).astype(jnp.int32), axis=1))
    firsts = (jnp.cumsum(loads) - loads).astype(jnp.int32)

    def per_expert(index, accum):
        begin = firsts[index].astype(jnp.int32)
        chosen = lax.dynamic_slice_in_dim(sorted_rows, begin, row_limit, 0)
        valid = jnp.arange(row_limit, dtype=jnp.int32) < loads[index]
        weight_in = w_in[index]
        hidden = jnp.maximum(jnp.dot(chosen, weight_in.T, preferred_element_type=jnp.float32), 0.0).astype(jnp.bfloat16)
        hidden_f = lax.optimization_barrier(hidden).astype(jnp.float32).reshape(row_limit, GROUP, FS)
        weight_out = w_out[index].astype(jnp.float32).reshape(GROUP, FS, D)
        pieces = jnp.einsum('rgf,gfd->rgd', hidden_f, weight_out)
        pieces = lax.optimization_barrier(pieces.astype(jnp.bfloat16)).astype(jnp.float32)
        summed = lax.optimization_barrier(jnp.sum(pieces, axis=1)).astype(jnp.bfloat16)
        summed = lax.optimization_barrier(summed).astype(jnp.float32)
        result = jnp.where(valid[:, None], summed, jnp.float32(0.0))
        current = lax.dynamic_slice_in_dim(accum, begin, row_limit, 0)
        return lax.dynamic_update_slice_in_dim(accum, current + result, begin, 0)
    accum = lax.fori_loop(0, EXPERTS, per_expert, jnp.zeros((count_all + row_limit, D), jnp.float32))
    expert_out = jnp.zeros((count_all, D), jnp.float32).at[order].set(accum[:count_all])
    scale = (keep.astype(jnp.float32) * route_prob).reshape(-1, 1)
    mixed = (state.reshape(-1, D) + scale * expert_out).astype(jnp.bfloat16)
    return mixed.reshape(UTT, TOKENS, D)
```

```python
import functools
import math

import jax
import jax.numpy as jnp
from jax import lax
from jax.experimental import pallas as pl
from jax.experimental.pallas import tpu as pltpu
from jax.sharding import PartitionSpec as P

D = 4096
HEADS = 32
KV_HEADS = 8
DH = 128
WIN = 128
CORES = 2
VMEM_LIMIT = 48 * 1024 * 1024


def attend_kernel(shards, blocks, rel_ref, q_ref, res_ref, gain_ref, *refs):
    kv_refs = refs[:shards]
    disp_refs = refs[shards : shards + blocks]
    state_ref = refs[shards + blocks]
    out_refs = refs[shards + blocks + 1 :]
    tok_count = q_ref.shape[0]
    groups = HEADS // KV_HEADS
    frames = kv_refs[0].shape[1]
    row = lax.broadcasted_iota(jnp.int32, (WIN, frames), 0)
    col = lax.broadcasted_iota(jnp.int32, (WIN, frames), 1)
    band = [None, None]
    for j in range(shards):
        pick = (col == row + rel_ref[j]).astype(jnp.bfloat16)
        for side in range(2):
            part = jnp.dot(pick, kv_refs[j][side], preferred_element_type=jnp.float32)
            band[side] = part if band[side] is None else band[side] + part
    keys_b = band[0].astype(jnp.bfloat16)
    values_b = band[1].astype(jnp.bfloat16)
    squares = jnp.zeros((tok_count, 1), jnp.float32)
    for g in range(KV_HEADS):
        key = keys_b[:, g * DH : (g + 1) * DH]
        value = values_b[:, g * DH : (g + 1) * DH]
        for h in range(g * groups, (g + 1) * groups):
            cols = slice(h * DH, (h + 1) * DH)
            scores = lax.dot_general(
                q_ref[:, cols], key, (((1,), (1,)), ((), ())), preferred_element_type=jnp.float32
            ) * (1.0 / math.sqrt(DH))
            weights = jnp.exp(scores - jnp.max(scores, axis=-1, keepdims=True))
            total = jnp.sum(weights, axis=-1, keepdims=True)
            context = jnp.dot(
                weights.astype(jnp.bfloat16), value, preferred_element_type=jnp.float32
            ) / total
            state = res_ref[:, cols].astype(jnp.float32) + context
            state_ref[:, cols] = state
            squares = squares + jnp.sum(state * state, axis=-1, keepdims=True)
    scale = lax.rsqrt(squares / D + 1e-06)
    normed = (state_ref[...] * scale * gain_ref[...]).astype(jnp.bfloat16)
    for disp_ref, out_ref in zip(disp_refs, out_refs):
        out_ref[...] = jnp.dot(
            disp_ref[...], normed, preferred_element_type=jnp.float32
        ).astype(jnp.bfloat16)


def attend(rel, query_rows, residual, gain, shards, dispatch):
    tok_count = query_rows.shape[0]
    vmem = pl.BlockSpec(memory_space=pltpu.VMEM)
    outs = [jax.ShapeDtypeStruct((tok_count, D), jnp.float32)]
    outs += [jax.ShapeDtypeStruct((d.shape[0], D), jnp.bfloat16) for d in dispatch]
    return pl.pallas_call(
        functools.partial(attend_kernel, len(shards), len(dispatch)),
        out_shape=outs,
        in_specs=[pl.BlockSpec(memory_space=pltpu.SMEM)]
        + [vmem] * (3 + len(shards) + len(dispatch)),
        out_specs=[vmem] * len(outs),
        compiler_params=pltpu.CompilerParams(vmem_limit_bytes=VMEM_LIMIT),
        cost_estimate=pl.CostEstimate(
            flops=6 * tok_count * D * WIN, bytes_accessed=6_000_000, transcendentals=HEADS * WIN * tok_count
        ),
        name="attend",
    )(rel, query_rows, residual, gain, *shards, *dispatch)


def combine_kernel(blocks, state_ref, scale_ref, *refs):
    total = None
    for j in range(blocks):
        part = lax.dot_general(
            refs[j][...],
            refs[blocks + j][...],
            (((1,), (0,)), ((), ())),
            preferred_element_type=jnp.float32,
        )
        total = part if total is None else total + part
    refs[2 * blocks][...] = (state_ref[...] + scale_ref[...] * total).astype(jnp.bfloat16)


def combine(state, scale, undo, returned):
    tok_count = state.shape[0]
    blocks = len(undo)
    vmem = pl.BlockSpec(memory_space=pltpu.VMEM)
    return pl.pallas_call(
        functools.partial(combine_kernel, blocks),
        out_shape=jax.ShapeDtypeStruct((tok_count, D), jnp.bfloat16),
        in_specs=[vmem] * (2 + 2 * blocks),
        out_specs=vmem,
        compiler_params=pltpu.CompilerParams(vmem_limit_bytes=VMEM_LIMIT),
        cost_estimate=pl.CostEstimate(
            flops=2 * tok_count * tok_count * D, bytes_accessed=4_000_000, transcendentals=0
        ),
        name="combine",
    )(state, scale, *undo, *returned)


def body(
    queries, dec_state, enc_kv, band_start, norm_gain, route_ids, keep, route_prob, w_in, w_out
):
    sections = lax.axis_size("section")
    seqs = lax.axis_size("seq")
    depth = lax.axis_size("expert")
    chips = sections // CORES
    assert chips == 2 and w_in.shape[0] == CORES
    s = lax.axis_index("section")
    q = lax.axis_index("seq")
    core = s % CORES

    def route(source_of):
        pairs = []
        for a in range(sections):
            for b in range(seqs):
                origin = source_of(b)
                if origin is not None:
                    pairs.append((((a - 1) % sections) * seqs + origin, a * seqs + b))
        return pairs

    frames = enc_kv.shape[2]
    block = enc_kv[:, 0]
    if seqs == 2:
        shards = [
            lax.ppermute(block, ("section", "seq"), route(lambda b: b)),
            lax.ppermute(block, ("section", "seq"), route(lambda b: 1 - b)),
        ]
        origins = [q, 1 - q]
    else:
        shards = [
            lax.ppermute(block, ("section", "seq"), route(lambda b: b)),
            lax.ppermute(block, ("section", "seq"), route(lambda b: b - 1 if b > 0 else None)),
            lax.ppermute(
                block, ("section", "seq"), route(lambda b: b + 1 if b < seqs - 1 else None)
            ),
        ]
        origins = [q, q - 1, q + 1]
    rel = jnp.stack([band_start[0, 0] - origin * frames for origin in origins]).astype(jnp.int32)

    def core_pairs():
        return [(a, a ^ 1) for a in range(sections)]

    def pooled(weights):
        mine = lax.dynamic_index_in_dim(weights, core, 0, keepdims=False)
        other = lax.dynamic_index_in_dim(weights, 1 - core, 0, keepdims=False)
        return jnp.concatenate([mine, lax.ppermute(other, "section", core_pairs())], axis=0)

    experts_of = route_ids[0, :, 0]
    tok_count = experts_of.shape[0]
    expert_count = seqs * CORES
    capacity = max(2, tok_count // expert_count)
    one_hot = (experts_of[:, None] == jnp.arange(expert_count, dtype=jnp.int32)[None, :]).astype(
        jnp.int32
    )
    slot_of = jnp.sum((jnp.cumsum(one_hot, axis=0) - one_hot) * one_hot, axis=1)
    kept = keep[0] == 1
    turns = [(dq, dc) for dq in range(seqs) for dc in range(CORES)]
    slots = jnp.arange(capacity, dtype=jnp.int32)
    dispatch, undo = [], []
    for dq, dc in turns:
        expert = ((q + dq) % seqs) * CORES + (core ^ dc)
        code = jnp.where(kept & (experts_of == expert), slot_of, -1)
        dispatch.append((slots[:, None] == code[None, :]).astype(jnp.bfloat16))
        undo.append((code[:, None] == slots[None, :]).astype(jnp.bfloat16))

    state, *outgoing = attend(
        rel, queries[0], dec_state[0], norm_gain[None, :], shards, dispatch
    )

    def move_pairs(dq, dc):
        return [
            (a * seqs + b, (a ^ dc) * seqs + (b + dq) % seqs)
            for a in range(sections)
            for b in range(seqs)
        ]

    def back(pairs):
        return [(b, a) for a, b in pairs]

    arrived = []
    for (dq, dc), rows in zip(turns, outgoing):
        if (dq, dc) == (0, 0):
            arrived.append(rows)
        else:
            arrived.append(lax.ppermute(rows, ("section", "seq"), move_pairs(dq, dc)))
    parts = [
        jnp.concatenate(arrived[:CORES], axis=0),
        jnp.concatenate(arrived[CORES:], axis=0),
    ]

    cycle = [(0, z) for z in range(depth)] + [(1, z) for z in reversed(range(depth))]
    count = len(cycle)

    def hop(rows, step):
        pairs = []
        for c in range(CORES):
            ids = [(x * CORES + c) * depth + z for x, z in cycle]
            pairs += [(ids[i], ids[(i + step) % count]) for i in range(count)]
        return lax.ppermute(rows, ("section", "expert"), pairs)

    unit_in = pooled(w_in)
    unit_out = pooled(w_out)

    def units(rows):
        hidden = lax.dot_general(
            rows, unit_in, (((1,), (1,)), ((), ())), preferred_element_type=jnp.float32
        )
        return jnp.maximum(hidden, 0.0).astype(jnp.bfloat16)

    def partial_sum(hidden, total=None):
        part = jnp.dot(hidden, unit_out, preferred_element_type=jnp.float32)
        if total is not None:
            if total.shape[0] < part.shape[0]:
                total = jnp.pad(total, ((0, part.shape[0] - total.shape[0]), (0, 0)))
            part = part + total.astype(jnp.float32)
        return part.astype(jnp.bfloat16)

    half = count // 2
    fore = [[rows] for rows in parts]
    rear = [[rows] for rows in parts]
    for _ in range(1, half):
        for p in range(2):
            fore[p].append(hop(fore[p][-1], 1))
            rear[p].append(hop(rear[p][-1], -1))
    cut = [rows.shape[0] // 2 for rows in parts]
    for p in (1, 0):
        fore[p].append(hop(fore[p][-1][: cut[p]], 1))
        rear[p].append(hop(rear[p][-1][cut[p] :], -1))

    fore_h = [[units(rows) for rows in fore[p]] for p in range(2)]
    rear_h = [[None] + [units(rows) for rows in rear[p][1:]] for p in range(2)]

    ahead = [None, None]
    behind = [None, None]
    for k in range(half, 0, -1):
        for p in (1, 0):
            if k == half:
                ahead[p] = hop(partial_sum(fore_h[p][k]), 1)
                behind[p] = hop(partial_sum(rear_h[p][k]), -1)
            elif k == half - 1:
                ahead[p] = hop(partial_sum(rear_h[p][k], ahead[p]), 1)
                part = jnp.dot(fore_h[p][k], unit_out, preferred_element_type=jnp.float32)
                total = jnp.pad(behind[p], ((cut[p], 0), (0, 0)))
                behind[p] = hop((part + total.astype(jnp.float32)).astype(jnp.bfloat16), -1)
            else:
                ahead[p] = hop(partial_sum(rear_h[p][k], ahead[p]), 1)
                behind[p] = hop(partial_sum(fore_h[p][k], behind[p]), -1)
    sums = []
    for p in range(2):
        own = jnp.dot(fore_h[p][0], unit_out, preferred_element_type=jnp.float32)
        sums.append(
            (own + ahead[p].astype(jnp.float32) + behind[p].astype(jnp.float32)).astype(
                jnp.bfloat16
            )
        )
    pieces = [sums[0][i * capacity : (i + 1) * capacity] for i in range(CORES)]
    pieces += [
        sums[1][i * capacity : (i + 1) * capacity] for i in range(len(turns) - CORES)
    ]
    returned = []
    for (dq, dc), rows in zip(turns, pieces):
        if (dq, dc) == (0, 0):
            returned.append(rows)
        else:
            returned.append(lax.ppermute(rows, ("section", "seq"), back(move_pairs(dq, dc))))
    scale = (keep[0].astype(jnp.float32) * route_prob[0])[:, None]
    return combine(state, scale, undo, returned)[None]


def solution(mesh):
    return jax.shard_map(
        body,
        mesh=mesh,
        in_specs=(
            P(("section", "expert"), "seq", None),
            P(("section", "expert"), "seq", None),
            P(None, ("section", "expert"), "seq", None),
            P(("section", "expert"), "seq"),
            P(),
            P(("section", "expert"), "seq", None),
            P(("section", "expert"), "seq"),
            P(("section", "expert"), "seq"),
            P("seq", ("section", "expert"), None),
            P("seq", ("section", "expert"), None),
        ),
        out_specs=P(("section", "expert"), "seq", None),
        check_vma=False,
    )
```

```python
import functools
import math

import jax
import jax.numpy as jnp
from jax import lax
from jax.experimental import pallas as pl
from jax.experimental.pallas import tpu as pltpu
from jax.sharding import PartitionSpec as P

D = 4096
HEADS = 32
KV_HEADS = 8
DH = 128
WIN = 128
CORES = 2
VMEM_LIMIT = 32 * 1024 * 1024
EXPERT_VMEM = 32 * 1024 * 1024


def attend_kernel(shards, blocks, rel_ref, q_ref, res_ref, gain_ref, *refs):
    kv_refs = refs[:shards]
    disp_refs = refs[shards : shards + blocks]
    state_ref = refs[shards + blocks]
    out_refs = refs[shards + blocks + 1 :]
    tok_count = q_ref.shape[0]
    groups = HEADS // KV_HEADS
    frames = kv_refs[0].shape[1]
    row = lax.broadcasted_iota(jnp.int32, (WIN, frames), 0)
    col = lax.broadcasted_iota(jnp.int32, (WIN, frames), 1)
    band = [None, None]
    for j in range(shards):
        pick = (col == row + rel_ref[j]).astype(jnp.bfloat16)
        for side in range(2):
            part = jnp.dot(pick, kv_refs[j][side], preferred_element_type=jnp.float32)
            band[side] = part if band[side] is None else band[side] + part
    keys_b = band[0].astype(jnp.bfloat16)
    values_b = band[1].astype(jnp.bfloat16)
    squares = jnp.zeros((tok_count, 1), jnp.float32)
    for g in range(KV_HEADS):
        key = keys_b[:, g * DH : (g + 1) * DH]
        value = values_b[:, g * DH : (g + 1) * DH]
        for h in range(g * groups, (g + 1) * groups):
            cols = slice(h * DH, (h + 1) * DH)
            scores = lax.dot_general(
                q_ref[:, cols], key, (((1,), (1,)), ((), ())), preferred_element_type=jnp.float32
            ) * (1.0 / math.sqrt(DH))
            weights = jnp.exp(scores - jnp.max(scores, axis=-1, keepdims=True))
            total = jnp.sum(weights, axis=-1, keepdims=True)
            context = jnp.dot(
                weights.astype(jnp.bfloat16), value, preferred_element_type=jnp.float32
            ) / total
            state = res_ref[:, cols].astype(jnp.float32) + context
            state_ref[:, cols] = state
            squares = squares + jnp.sum(state * state, axis=-1, keepdims=True)
    scale = lax.rsqrt(squares / D + 1e-06)
    normed = (state_ref[...] * scale * gain_ref[...]).astype(jnp.bfloat16)
    for disp_ref, out_ref in zip(disp_refs, out_refs):
        out_ref[...] = jnp.dot(
            disp_ref[...], normed, preferred_element_type=jnp.float32
        ).astype(jnp.bfloat16)


def attend(rel, query_rows, residual, gain, shards, dispatch):
    tok_count = query_rows.shape[0]
    vmem = pl.BlockSpec(memory_space=pltpu.VMEM)
    outs = [jax.ShapeDtypeStruct((tok_count, D), jnp.float32)]
    outs += [jax.ShapeDtypeStruct((d.shape[0], D), jnp.bfloat16) for d in dispatch]
    return pl.pallas_call(
        functools.partial(attend_kernel, len(shards), len(dispatch)),
        out_shape=outs,
        in_specs=[pl.BlockSpec(memory_space=pltpu.SMEM)]
        + [pl.BlockSpec()] * (3 + len(shards) + len(dispatch)),
        out_specs=[vmem] * len(outs),
        compiler_params=pltpu.CompilerParams(vmem_limit_bytes=VMEM_LIMIT),
        cost_estimate=pl.CostEstimate(
            flops=6 * tok_count * D * WIN, bytes_accessed=6_000_000, transcendentals=HEADS * WIN * tok_count
        ),
        name="attend",
    )(rel, query_rows, residual, gain, *shards, *dispatch)


def expert_kernel(count, steps, *refs):
    x_refs = refs[:count]
    in_refs = refs[count : count + 2]
    out_w_refs = refs[count + 2 : count + 4]
    out_refs = refs[count + 4 : 2 * count + 4]
    acc_refs = refs[2 * count + 4 :]
    i = pl.program_id(0)
    rows = [ref.shape[0] for ref in x_refs]
    joined = all(r % 16 == 0 for r in rows)

    @pl.when(i < steps)
    def _():
        weight = jnp.concatenate([ref[...] for ref in in_refs], axis=0)
        if joined:
            groups = [jnp.concatenate([ref[...] for ref in x_refs], axis=0)]
        else:
            groups = [ref[...] for ref in x_refs]
        for rows_b, acc_ref in zip(groups, acc_refs):
            part = lax.dot_general(
                rows_b, weight, (((1,), (1,)), ((), ())), preferred_element_type=jnp.float32
            )

            @pl.when(i == 0)
            def _():
                acc_ref[...] = part

            @pl.when(i > 0)
            def _():
                acc_ref[...] += part

    @pl.when(i >= steps)
    def _():
        weight = jnp.concatenate([ref[...] for ref in out_w_refs], axis=0)
        begin = 0
        for j, acc_ref in enumerate(acc_refs):
            hidden = jnp.maximum(acc_ref[...], 0.0).astype(jnp.bfloat16)
            part = jnp.dot(hidden, weight, preferred_element_type=jnp.float32).astype(jnp.bfloat16)
            if joined:
                for r, out_ref in zip(rows, out_refs):
                    out_ref[...] = part[begin : begin + r]
                    begin += r
            else:
                out_refs[j][...] = part


def expert_sums(parts, unit_in, unit_out, steps=2):
    count = len(parts)
    rows = [x.shape[0] for x in parts]
    width = D // steps
    units = sum(w.shape[0] for w in unit_in)
    first = lambda i: (0, jnp.minimum(i, steps - 1))
    second = lambda i: (0, jnp.maximum(i - steps, 0))
    if all(r % 16 == 0 for r in rows):
        scratch = [pltpu.VMEM((sum(rows), units), jnp.float32)]
    else:
        scratch = [pltpu.VMEM((r, units), jnp.float32) for r in rows]
    return pl.pallas_call(
        functools.partial(expert_kernel, count, steps),
        grid=(2 * steps,),
        out_shape=[jax.ShapeDtypeStruct((r, D), jnp.bfloat16) for r in rows],
        in_specs=[pl.BlockSpec((r, width), first) for r in rows]
        + [pl.BlockSpec((w.shape[0], width), first) for w in unit_in]
        + [pl.BlockSpec((w.shape[0], width), second) for w in unit_out],
        out_specs=[pl.BlockSpec((r, width), second) for r in rows],
        scratch_shapes=scratch,
        compiler_params=pltpu.CompilerParams(vmem_limit_bytes=EXPERT_VMEM),
        cost_estimate=pl.CostEstimate(
            flops=4 * sum(rows) * units * D,
            bytes_accessed=4 * D * (units + sum(rows)),
            transcendentals=0,
        ),
        name="expert",
    )(*parts, *unit_in, *unit_out)


def combine_kernel(blocks, state_ref, scale_ref, *refs):
    total = None
    for j in range(blocks):
        part = lax.dot_general(
            refs[j][...],
            refs[blocks + j][...],
            (((1,), (0,)), ((), ())),
            preferred_element_type=jnp.float32,
        )
        total = part if total is None else total + part
    refs[2 * blocks][...] = (state_ref[...] + scale_ref[...] * total).astype(jnp.bfloat16)


def combine(state, scale, undo, returned):
    tok_count = state.shape[0]
    blocks = len(undo)
    vmem = pl.BlockSpec(memory_space=pltpu.VMEM)
    return pl.pallas_call(
        functools.partial(combine_kernel, blocks),
        out_shape=jax.ShapeDtypeStruct((tok_count, D), jnp.bfloat16),
        in_specs=[vmem] * (2 + 2 * blocks),
        out_specs=vmem,
        compiler_params=pltpu.CompilerParams(vmem_limit_bytes=VMEM_LIMIT),
        cost_estimate=pl.CostEstimate(
            flops=2 * tok_count * tok_count * D, bytes_accessed=4_000_000, transcendentals=0
        ),
        name="combine",
    )(state, scale, *undo, *returned)


def body(
    queries, dec_state, enc_kv, band_start, norm_gain, route_ids, keep, route_prob, w_in, w_out
):
    sections = lax.axis_size("section")
    seqs = lax.axis_size("seq")
    depth = lax.axis_size("expert")
    chips = sections // CORES
    assert chips == 2 and w_in.shape[0] == CORES
    s = lax.axis_index("section")
    q = lax.axis_index("seq")
    core = s % CORES

    def route(source_of):
        pairs = []
        for a in range(sections):
            for b in range(seqs):
                origin = source_of(b)
                if origin is not None:
                    pairs.append((((a - 1) % sections) * seqs + origin, a * seqs + b))
        return pairs

    frames = enc_kv.shape[2]
    block = enc_kv[:, 0]
    if seqs == 2:
        shards = [
            lax.ppermute(block, ("section", "seq"), route(lambda b: b)),
            lax.ppermute(block, ("section", "seq"), route(lambda b: 1 - b)),
        ]
        origins = [q, 1 - q]
    else:
        shards = [
            lax.ppermute(block, ("section", "seq"), route(lambda b: b)),
            lax.ppermute(block, ("section", "seq"), route(lambda b: b - 1 if b > 0 else None)),
            lax.ppermute(
                block, ("section", "seq"), route(lambda b: b + 1 if b < seqs - 1 else None)
            ),
        ]
        origins = [q, q - 1, q + 1]
    rel = jnp.stack([band_start[0, 0] - origin * frames for origin in origins]).astype(jnp.int32)

    def core_pairs():
        return [(a, a ^ 1) for a in range(sections)]

    def pooled(weights):
        mine = lax.dynamic_index_in_dim(weights, core, 0, keepdims=False)
        other = lax.dynamic_index_in_dim(weights, 1 - core, 0, keepdims=False)
        return [mine, lax.ppermute(other, "section", core_pairs())]

    experts_of = route_ids[0, :, 0]
    tok_count = experts_of.shape[0]
    expert_count = seqs * CORES
    capacity = max(2, tok_count // expert_count)
    one_hot = (experts_of[:, None] == jnp.arange(expert_count, dtype=jnp.int32)[None, :]).astype(
        jnp.int32
    )
    slot_of = jnp.sum((jnp.cumsum(one_hot, axis=0) - one_hot) * one_hot, axis=1)
    kept = keep[0] == 1
    turns = [(dq, dc) for dq in range(seqs) for dc in range(CORES)]
    slots = jnp.arange(capacity, dtype=jnp.int32)
    dispatch, undo = [], []
    for dq, dc in turns:
        expert = ((q + dq) % seqs) * CORES + (core ^ dc)
        code = jnp.where(kept & (experts_of == expert), slot_of, -1)
        dispatch.append((slots[:, None] == code[None, :]).astype(jnp.bfloat16))
        undo.append((code[:, None] == slots[None, :]).astype(jnp.bfloat16))

    state, *outgoing = attend(
        rel, queries[0], dec_state[0], norm_gain[None, :], shards, dispatch
    )

    def move_pairs(dq, dc):
        return [
            (a * seqs + b, (a ^ dc) * seqs + (b + dq) % seqs)
            for a in range(sections)
            for b in range(seqs)
        ]

    def back(pairs):
        return [(b, a) for a, b in pairs]

    def swap(rows, dq, dc):
        return lax.ppermute(rows, ("section", "seq"), move_pairs(dq, dc))

    near = [outgoing[0]] + [swap(rows, 0, dc) for dc, rows in zip(range(1, CORES), outgoing[1:])]
    near, far = lax.optimization_barrier((near, outgoing[CORES:]))
    far = [swap(rows, dq, dc) for (dq, dc), rows in zip(turns[CORES:], far)]
    parts = [jnp.concatenate(near, axis=0), jnp.concatenate(far, axis=0)]

    cycle = [(0, z) for z in range(depth)] + [(1, z) for z in reversed(range(depth))]
    count = len(cycle)

    def hop(rows, step):
        pairs = []
        for c in range(CORES):
            ids = [(x * CORES + c) * depth + z for x, z in cycle]
            pairs += [(ids[i], ids[(i + step) % count]) for i in range(count)]
        return lax.ppermute(rows, ("section", "expert"), pairs)

    unit_in = pooled(w_in)
    unit_out = pooled(w_out)

    half = count // 2
    fore = [[rows] for rows in parts]
    rear = [[rows] for rows in parts]
    for _ in range(1, half):
        for p in range(2):
            fore[p].append(hop(fore[p][-1], 1))
            rear[p].append(hop(rear[p][-1], -1))
    sizes = [rows.shape[0] for rows in parts]
    cut = [min(sizes[0], (sizes[0] // 2 + 15) // 16 * 16), sizes[1] // 2 // 16 * 16]
    for p in (1, 0):
        if cut[p] > 0:
            fore[p].append(hop(fore[p][-1][: cut[p]], 1))
        if cut[p] < sizes[p]:
            rear[p].append(hop(rear[p][-1][cut[p] :], -1))

    own = expert_sums(parts, unit_in, unit_out)
    ahead_part, behind_part = [{}, {}], [{}, {}]
    for k in range(1, half):
        got = expert_sums([fore[0][k], fore[1][k], rear[0][k], rear[1][k]], unit_in, unit_out)
        for p in range(2):
            behind_part[p][k] = got[p]
            ahead_part[p][k] = got[2 + p]
    for p in (1, 0):
        rows = fore[p][half:] + rear[p][half:]
        got = list(expert_sums(rows, unit_in, unit_out))
        if cut[p] > 0:
            ahead_part[p][half] = got.pop(0)
        if cut[p] < sizes[p]:
            behind_part[p][half] = got.pop(0)

    def added(part, total, before):
        if total is None:
            return part
        after = part.shape[0] - before - total.shape[0]
        total = jnp.pad(total, ((before, after), (0, 0)))
        return (part.astype(jnp.float32) + total.astype(jnp.float32)).astype(jnp.bfloat16)

    ahead, behind = [None, None], [None, None]
    for k in range(half, 0, -1):
        for p in (1, 0):
            if k in ahead_part[p]:
                ahead[p] = hop(added(ahead_part[p][k], ahead[p], 0), 1)
            if k in behind_part[p]:
                before = cut[p] if k == half - 1 else 0
                behind[p] = hop(added(behind_part[p][k], behind[p], before), -1)
    sums = [
        (
            own[p].astype(jnp.float32)
            + ahead[p].astype(jnp.float32)
            + behind[p].astype(jnp.float32)
        ).astype(jnp.bfloat16)
        for p in range(2)
    ]
    pieces = [sums[0][i * capacity : (i + 1) * capacity] for i in range(CORES)]
    pieces += [
        sums[1][i * capacity : (i + 1) * capacity] for i in range(len(turns) - CORES)
    ]
    returned = []
    for (dq, dc), rows in zip(turns, pieces):
        if (dq, dc) == (0, 0):
            returned.append(rows)
        else:
            returned.append(lax.ppermute(rows, ("section", "seq"), back(move_pairs(dq, dc))))
    scale = (keep[0].astype(jnp.float32) * route_prob[0])[:, None]
    return combine(state, scale, undo, returned)[None]


def solution(mesh):
    return jax.shard_map(
        body,
        mesh=mesh,
        in_specs=(
            P(("section", "expert"), "seq", None),
            P(("section", "expert"), "seq", None),
            P(None, ("section", "expert"), "seq", None),
            P(("section", "expert"), "seq"),
            P(),
            P(("section", "expert"), "seq", None),
            P(("section", "expert"), "seq"),
            P(("section", "expert"), "seq"),
            P("seq", ("section", "expert"), None),
            P("seq", ("section", "expert"), None),
        ),
        out_specs=P(("section", "expert"), "seq", None),
        check_vma=False,
    )
```

```python
import functools
import math

import jax
import jax.numpy as jnp
from jax import lax
from jax.experimental import pallas as pl
from jax.experimental.pallas import tpu as pltpu
from jax.sharding import PartitionSpec as P

D = 4096
HEADS = 32
KV_HEADS = 8
DH = 128
WIN = 128
CORES = 2
VMEM_LIMIT = 16 * 1024 * 1024
EXPERT_VMEM = 8 * 1024 * 1024
SPAN = 1024


def attend_kernel(shards, blocks, rel_ref, q_ref, res_ref, gain_ref, *refs):
    kv_refs = refs[:shards]
    disp_refs = refs[shards : shards + blocks]
    state_ref = refs[shards + blocks]
    out_refs = refs[shards + blocks + 1 :]
    tok_count = q_ref.shape[0]
    groups = HEADS // KV_HEADS
    frames = kv_refs[0].shape[1]
    row = lax.broadcasted_iota(jnp.int32, (WIN, frames), 0)
    col = lax.broadcasted_iota(jnp.int32, (WIN, frames), 1)
    band = [None, None]
    for j in range(shards):
        pick = (col == row + rel_ref[j]).astype(jnp.bfloat16)
        for side in range(2):
            part = jnp.dot(pick, kv_refs[j][side], preferred_element_type=jnp.float32)
            band[side] = part if band[side] is None else band[side] + part
    keys_b = band[0].astype(jnp.bfloat16)
    values_b = band[1].astype(jnp.bfloat16)
    squares = jnp.zeros((tok_count, DH), jnp.float32)
    for g in range(KV_HEADS):
        key = keys_b[:, g * DH : (g + 1) * DH]
        value = values_b[:, g * DH : (g + 1) * DH]
        heads = [slice(h * DH, (h + 1) * DH) for h in range(g * groups, (g + 1) * groups)]
        grouped = jnp.concatenate([q_ref[:, cols] for cols in heads], axis=0)
        scores = lax.dot_general(
            grouped, key, (((1,), (1,)), ((), ())), preferred_element_type=jnp.float32
        ) * (1.0 / math.sqrt(DH))
        weights = jnp.exp(scores - jnp.max(scores, axis=-1, keepdims=True))
        total = jnp.sum(weights, axis=-1, keepdims=True)
        context = jnp.dot(
            weights.astype(jnp.bfloat16), value, preferred_element_type=jnp.float32
        ) / total
        for i, cols in enumerate(heads):
            state = res_ref[:, cols].astype(jnp.float32) + context[i * tok_count : (i + 1) * tok_count]
            state_ref[:, cols] = state
            squares = squares + state * state
    squares = jnp.sum(squares, axis=-1, keepdims=True)
    scale = lax.rsqrt(squares / D + 1e-06)
    normed = (state_ref[...] * scale * gain_ref[...]).astype(jnp.bfloat16)
    for disp_ref, out_ref in zip(disp_refs, out_refs):
        out_ref[...] = jnp.dot(
            disp_ref[...], normed, preferred_element_type=jnp.float32
        ).astype(jnp.bfloat16)


def attend(rel, query_rows, residual, gain, shards, dispatch):
    tok_count = query_rows.shape[0]
    vmem = pl.BlockSpec(memory_space=pltpu.VMEM)
    outs = [jax.ShapeDtypeStruct((tok_count, D), jnp.float32)]
    outs += [jax.ShapeDtypeStruct((d.shape[0], D), jnp.bfloat16) for d in dispatch]
    return pl.pallas_call(
        functools.partial(attend_kernel, len(shards), len(dispatch)),
        out_shape=outs,
        in_specs=[pl.BlockSpec(memory_space=pltpu.SMEM)]
        + [vmem] * (3 + len(shards) + len(dispatch)),
        out_specs=[vmem] * len(outs),
        compiler_params=pltpu.CompilerParams(vmem_limit_bytes=VMEM_LIMIT),
        cost_estimate=pl.CostEstimate(
            flops=6 * tok_count * D * WIN, bytes_accessed=6_000_000, transcendentals=HEADS * WIN * tok_count
        ),
        name="attend",
    )(rel, query_rows, residual, gain, *shards, *dispatch)


def expert_kernel(count, *refs):
    x_refs = refs[:count]
    in_ref, out_w_ref = refs[count], refs[count + 1]
    out_refs = refs[count + 2 :]
    joined = all(ref.shape[0] % 16 == 0 for ref in x_refs)
    groups = [x_refs] if joined else [[ref] for ref in x_refs]
    targets = [out_refs] if joined else [[ref] for ref in out_refs]
    for sources, outs in zip(groups, targets):
        rows_b = jnp.concatenate([ref[...] for ref in sources], axis=0)
        hidden = lax.dot_general(
            rows_b, in_ref[...], (((1,), (1,)), ((), ())), preferred_element_type=jnp.float32
        )
        hidden = jnp.maximum(hidden, 0.0).astype(jnp.bfloat16)
        for at in range(0, D, SPAN):
            cols = slice(at, at + SPAN)
            part = jnp.dot(
                hidden, out_w_ref[:, cols], preferred_element_type=jnp.float32
            ).astype(jnp.bfloat16)
            begin = 0
            for out_ref in outs:
                out_ref[:, cols] = part[begin : begin + out_ref.shape[0]]
                begin += out_ref.shape[0]


def pick_kernel(core_ref, in_ref, out_w_ref, pair_in_ref, pair_out_ref, sems):
    other = 1 - core_ref[0]
    copies = [
        pltpu.make_async_copy(in_ref.at[other], pair_in_ref, sems.at[0]),
        pltpu.make_async_copy(out_w_ref.at[other], pair_out_ref, sems.at[1]),
    ]
    for copy in copies:
        copy.start()
    for copy in copies:
        copy.wait()


def pool_kernel(core_ref, in_ref, out_w_ref, pair_in_ref, pair_out_ref, unit_in_ref, unit_out_ref, sems):
    core = core_ref[0]
    units = pair_in_ref.shape[0]
    copies = []
    sources = [
        (in_ref.at[core], pair_in_ref, unit_in_ref),
        (out_w_ref.at[core], pair_out_ref, unit_out_ref),
    ]
    for mine, other, target in sources:
        for at, source in enumerate((mine, other)):
            copies.append(
                pltpu.make_async_copy(
                    source, target.at[pl.ds(at * units, units)], sems.at[len(copies)]
                )
            )
    for copy in copies:
        copy.start()
    for copy in copies:
        copy.wait()


def staged(kernel, core, arrays, rows, copies, name):
    anywhere = pl.BlockSpec(memory_space=pl.ANY)
    vmem = pl.BlockSpec(memory_space=pltpu.VMEM)
    return pl.pallas_call(
        kernel,
        out_shape=[rows_like(rows), rows_like(rows)],
        in_specs=[pl.BlockSpec(memory_space=pltpu.SMEM)] + [anywhere] * len(arrays),
        out_specs=[vmem, vmem],
        scratch_shapes=[pltpu.SemaphoreType.DMA((copies,))],
        compiler_params=pltpu.CompilerParams(vmem_limit_bytes=EXPERT_VMEM),
        cost_estimate=pl.CostEstimate(
            flops=0, bytes_accessed=4 * rows * D * 2, transcendentals=0
        ),
        name=name,
    )(core, *arrays)


def expert_sums(parts, unit_in, unit_out):
    rows = [x.shape[0] for x in parts]
    units = unit_in.shape[0]
    vmem = pl.BlockSpec(memory_space=pltpu.VMEM)
    return pl.pallas_call(
        functools.partial(expert_kernel, len(parts)),
        out_shape=[jax.ShapeDtypeStruct((r, D), jnp.bfloat16) for r in rows],
        in_specs=[vmem] * (len(parts) + 2),
        out_specs=[vmem] * len(parts),
        compiler_params=pltpu.CompilerParams(vmem_limit_bytes=EXPERT_VMEM),
        cost_estimate=pl.CostEstimate(
            flops=4 * sum(rows) * units * D,
            bytes_accessed=4 * D * (units + sum(rows)),
            transcendentals=0,
        ),
        name="expert",
    )(*parts, unit_in, unit_out)


def local(kernel, outs, *args, name):
    vmem = pl.BlockSpec(memory_space=pltpu.VMEM)
    moved = sum(x.size * x.dtype.itemsize for x in (*args, *outs))
    return pl.pallas_call(
        kernel,
        out_shape=outs,
        in_specs=[vmem] * len(args),
        out_specs=[vmem] * len(outs),
        compiler_params=pltpu.CompilerParams(vmem_limit_bytes=EXPERT_VMEM),
        cost_estimate=pl.CostEstimate(
            flops=moved // 2, bytes_accessed=moved, transcendentals=0
        ),
        name=name,
    )(*args)


def rows_like(rows):
    return jax.ShapeDtypeStruct((rows, D), jnp.bfloat16)


def join_slots(stayed, crossed):
    capacity = stayed[0].shape[0]
    if capacity % 8:
        return [
            jnp.concatenate([rows, crossed[i * capacity : (i + 1) * capacity]], axis=0)
            for i, rows in enumerate(stayed)
        ]

    def kernel(*refs):
        count = len(stayed)
        other = refs[count][...].astype(jnp.float32)
        for i in range(count):
            pair = [refs[i][...].astype(jnp.float32), other[i * capacity : (i + 1) * capacity]]
            refs[count + 1 + i][...] = jnp.concatenate(pair, axis=0).astype(jnp.bfloat16)

    outs = [rows_like(2 * capacity) for _ in stayed]
    return local(kernel, outs, *stayed, crossed, name="join_slots")


def split_rows(fore_rows, rear_rows, cut):
    size = fore_rows.shape[0]

    def kernel(fore_ref, rear_ref, *out_refs):
        out_refs = list(out_refs)
        if cut > 0:
            out_refs.pop(0)[...] = fore_ref[:cut, :]
        if cut < size:
            out_refs.pop(0)[...] = rear_ref[cut:, :]

    outs = [rows_like(rows) for rows in (cut, size - cut) if rows > 0]
    return local(kernel, outs, fore_rows, rear_rows, name="split_rows")


def add_sums(ahead_part, behind_part, ahead, behind, cut):
    size = ahead_part.shape[0]

    def filled(rows, before):
        rows = rows.astype(jnp.float32)
        edges = [jnp.zeros((before, D), jnp.float32)] if before else []
        edges.append(rows)
        after = size - before - rows.shape[0]
        if after:
            edges.append(jnp.zeros((after, D), jnp.float32))
        return jnp.concatenate(edges, axis=0) if len(edges) > 1 else rows

    totals = [x for x in (ahead, behind) if x is not None]

    def kernel(*refs):
        refs = list(refs)
        sums = [refs.pop(0)[...].astype(jnp.float32), refs.pop(0)[...].astype(jnp.float32)]
        if ahead is not None:
            sums[0] = sums[0] + filled(refs.pop(0)[...], 0)
        if behind is not None:
            sums[1] = sums[1] + filled(refs.pop(0)[...], size - behind.shape[0])
        for out_ref, total in zip(refs, sums):
            out_ref[...] = total.astype(jnp.bfloat16)

    outs = [rows_like(size), rows_like(size)]
    return local(kernel, outs, ahead_part, behind_part, *totals, name="add_sums")


def finish_sums(own, ahead, behind):
    def kernel(own_ref, ahead_ref, behind_ref, out_ref):
        total = own_ref[...].astype(jnp.float32) + ahead_ref[...].astype(jnp.float32)
        out_ref[...] = (total + behind_ref[...].astype(jnp.float32)).astype(jnp.bfloat16)

    return local(kernel, [rows_like(own.shape[0])], own, ahead, behind, name="finish_sums")[0]


def combine_kernel(blocks, state_ref, scale_ref, *refs):
    total = None
    for j in range(blocks):
        part = lax.dot_general(
            refs[j][...],
            refs[blocks + j][...],
            (((1,), (0,)), ((), ())),
            preferred_element_type=jnp.float32,
        )
        total = part if total is None else total + part
    refs[2 * blocks][...] = (state_ref[...] + scale_ref[...] * total).astype(jnp.bfloat16)


def combine(state, scale, undo, returned):
    tok_count = state.shape[0]
    blocks = len(undo)
    vmem = pl.BlockSpec(memory_space=pltpu.VMEM)
    return pl.pallas_call(
        functools.partial(combine_kernel, blocks),
        out_shape=jax.ShapeDtypeStruct((tok_count, D), jnp.bfloat16),
        in_specs=[vmem] * (2 + 2 * blocks),
        out_specs=vmem,
        compiler_params=pltpu.CompilerParams(vmem_limit_bytes=EXPERT_VMEM),
        cost_estimate=pl.CostEstimate(
            flops=2 * tok_count * tok_count * D, bytes_accessed=4_000_000, transcendentals=0
        ),
        name="combine",
    )(state, scale, *undo, *returned)


def body(
    queries, dec_state, enc_kv, band_start, norm_gain, route_ids, keep, route_prob, w_in, w_out
):
    sections = lax.axis_size("section")
    seqs = lax.axis_size("seq")
    depth = lax.axis_size("expert")
    chips = sections // CORES
    assert chips == 2 and w_in.shape[0] == CORES
    s = lax.axis_index("section")
    q = lax.axis_index("seq")
    core = s % CORES

    def route(source_of):
        pairs = []
        for a in range(sections):
            for b in range(seqs):
                origin = source_of(b)
                if origin is not None:
                    pairs.append((((a - 1) % sections) * seqs + origin, a * seqs + b))
        return pairs

    frames = enc_kv.shape[2]
    block = enc_kv[:, 0]
    if seqs == 2:
        shards = [
            lax.ppermute(block, ("section", "seq"), route(lambda b: b)),
            lax.ppermute(block, ("section", "seq"), route(lambda b: 1 - b)),
        ]
        origins = [q, 1 - q]
    else:
        shards = [
            lax.ppermute(block, ("section", "seq"), route(lambda b: b)),
            lax.ppermute(block, ("section", "seq"), route(lambda b: b - 1 if b > 0 else None)),
            lax.ppermute(
                block, ("section", "seq"), route(lambda b: b + 1 if b < seqs - 1 else None)
            ),
        ]
        origins = [q, q - 1, q + 1]
    rel = jnp.stack([band_start[0, 0] - origin * frames for origin in origins]).astype(jnp.int32)

    def core_pairs():
        return [(a, a ^ 1) for a in range(sections)]

    core_at = core.astype(jnp.int32)[None]
    share = w_in.shape[1]
    pair_units = staged(pick_kernel, core_at, [w_in, w_out], share, 2, "pick_units")
    rel, pair_units = lax.optimization_barrier((rel, pair_units))
    pair_units = [lax.ppermute(rows, "section", core_pairs()) for rows in pair_units]

    experts_of = route_ids[0, :, 0]
    tok_count = experts_of.shape[0]
    expert_count = seqs * CORES
    capacity = max(2, tok_count // expert_count)
    one_hot = (experts_of[:, None] == jnp.arange(expert_count, dtype=jnp.int32)[None, :]).astype(
        jnp.int32
    )
    slot_of = jnp.sum((jnp.cumsum(one_hot, axis=0) - one_hot) * one_hot, axis=1)
    kept = keep[0] == 1
    turns = [(dq, dc) for dq in range(seqs) for dc in range(CORES)]
    slots = jnp.arange(capacity, dtype=jnp.int32)
    dispatch, undo = [], []
    block_slots = jnp.arange(CORES * capacity, dtype=jnp.int32)
    for dq, dc in turns:
        named = ((q + dq) % seqs) * CORES + (core ^ dc)
        code = jnp.where(kept & (experts_of == named), slot_of, -1)
        dispatch.append((slots[:, None] == code[None, :]).astype(jnp.bfloat16))
        code = jnp.where(code >= 0, code + dc * capacity, -1)
        undo.append((code[:, None] == block_slots[None, :]).astype(jnp.bfloat16))
    scale = (keep[0].astype(jnp.float32) * route_prob[0])[:, None]

    crossing = jnp.concatenate(
        [rows for (dq, dc), rows in zip(turns, dispatch) if dc == 1], axis=0
    )
    staying = [rows for (dq, dc), rows in zip(turns, dispatch) if dc == 0]
    rel, crossing, staying, undo, scale = lax.optimization_barrier(
        (rel, crossing, staying, undo, scale)
    )
    state, crossed, *stayed = attend(
        rel, queries[0], dec_state[0], norm_gain[None, :], shards, [crossing] + staying
    )

    def core_swap(rows):
        return lax.ppermute(rows, "section", core_pairs())

    def seq_move(rows, step):
        return lax.ppermute(rows, "seq", [(b, (b + step) % seqs) for b in range(seqs)])

    slot_blocks = join_slots(stayed, core_swap(crossed))
    moved = [seq_move(slot_blocks[dq], dq) for dq in range(1, seqs)]
    parts = [slot_blocks[0], moved[0] if seqs == 2 else jnp.concatenate(moved, axis=0)]

    unit_in, unit_out = staged(
        pool_kernel, core_at, [w_in, w_out, *pair_units], CORES * share, 4, "pool_units"
    )
    parts[1], unit_in, unit_out = lax.optimization_barrier((parts[1], unit_in, unit_out))

    cycle = [(0, z) for z in range(depth)] + [(1, z) for z in reversed(range(depth))]
    count = len(cycle)

    def hop(rows, step):
        pairs = []
        for c in range(CORES):
            ids = [(x * CORES + c) * depth + z for x, z in cycle]
            pairs += [(ids[i], ids[(i + step) % count]) for i in range(count)]
        return lax.ppermute(rows, ("section", "expert"), pairs)

    half = count // 2
    sizes = [rows.shape[0] for rows in parts]
    cut = [min(sizes[0], (sizes[0] // 2 + 15) // 16 * 16), sizes[1] // 2 // 16 * 16]
    fore = [[rows] for rows in parts]
    rear = [[rows] for rows in parts]
    sums = {}

    def after(key, rows):
        if key in sums:
            rows, sums[key] = lax.optimization_barrier((rows, sums[key]))
        return rows

    for k in range(1, half):
        for p in range(2):
            rows = after(k - 2, lax.optimization_barrier((fore[p][-1], rear[p][-1])))
            fore[p].append(hop(rows[0], 1))
            rear[p].append(hop(rows[1], -1))
        rows = [fore[0][k], fore[1][k], rear[0][k], rear[1][k]]
        sums[k] = expert_sums(rows, unit_in, unit_out)
    for p in (1, 0):
        rows = split_rows(*after(half - 2, (fore[p][-1], rear[p][-1])), cut[p])
        if cut[p] > 0:
            fore[p].append(hop(rows[0], 1))
        if cut[p] < sizes[p]:
            rear[p].append(hop(rows[-1], -1))
    ahead_part, behind_part = [{}, {}], [{}, {}]
    for p in (1, 0):
        rows = fore[p][half:] + rear[p][half:]
        if p == 1:
            rows = after(half - 1, rows)
        got = list(expert_sums(rows, unit_in, unit_out))
        if cut[p] > 0:
            ahead_part[p][half] = got.pop(0)
        if cut[p] < sizes[p]:
            behind_part[p][half] = got.pop(0)
    for k in range(1, half):
        for p in range(2):
            behind_part[p][k] = sums[k][p]
            ahead_part[p][k] = sums[k][2 + p]

    ahead, behind = [None, None], [None, None]
    for p in (1, 0):
        if half in ahead_part[p]:
            ahead[p] = hop(ahead_part[p][half], 1)
        if half in behind_part[p]:
            behind[p] = hop(behind_part[p][half], -1)
    for k in range(half - 1, 0, -1):
        for p in (1, 0):
            if k == half - 1 and p == 1:
                ahead[p], parts = lax.optimization_barrier((ahead[p], parts))
                sums["own"] = expert_sums(parts, unit_in, unit_out)
            totals = add_sums(
                ahead_part[p][k], behind_part[p][k], ahead[p], behind[p], cut[p]
            )
            if k == 1:
                totals = after("own", totals)
            ahead[p], behind[p] = hop(totals[0], 1), hop(totals[1], -1)
    done = [finish_sums(sums["own"][p], ahead[p], behind[p]) for p in range(2)]

    width = CORES * capacity
    if seqs == 2:
        far = [done[1]]
    else:
        far = [done[1][i * width : (i + 1) * width] for i in range(seqs - 1)]
    returned = []
    for dq, rows in enumerate([done[0]] + far):
        rows = seq_move(rows, -dq) if dq else rows
        returned += [rows, core_swap(rows)]
    return combine(state, scale, undo, returned)[None]


def solution(mesh):
    return jax.shard_map(
        body,
        mesh=mesh,
        in_specs=(
            P(("section", "expert"), "seq", None),
            P(("section", "expert"), "seq", None),
            P(None, ("section", "expert"), "seq", None),
            P(("section", "expert"), "seq"),
            P(),
            P(("section", "expert"), "seq", None),
            P(("section", "expert"), "seq"),
            P(("section", "expert"), "seq"),
            P("seq", ("section", "expert"), None),
            P("seq", ("section", "expert"), None),
        ),
        out_specs=P(("section", "expert"), "seq", None),
        check_vma=False,
    )
```

```python
import functools
import math

import jax
import jax.numpy as jnp
from jax import lax
from jax.experimental import pallas as pl
from jax.experimental.pallas import tpu as pltpu
from jax.sharding import PartitionSpec as P

D = 4096
HEADS = 32
KV_HEADS = 8
DH = 128
WIN = 128
CORES = 2
VMEM_LIMIT = 16 * 1024 * 1024
EXPERT_VMEM = 8 * 1024 * 1024
SPAN = 1024


def attend_kernel(shards, blocks, rel_ref, q_ref, res_ref, gain_ref, *refs):
    kv_refs = refs[:shards]
    disp_refs = refs[shards : shards + blocks]
    state_ref = refs[shards + blocks]
    out_refs = refs[shards + blocks + 1 :]
    tok_count = q_ref.shape[0]
    groups = HEADS // KV_HEADS
    frames = kv_refs[0].shape[1]
    row = lax.broadcasted_iota(jnp.int32, (WIN, frames), 0)
    col = lax.broadcasted_iota(jnp.int32, (WIN, frames), 1)
    band = [None, None]
    for j in range(shards):
        pick = (col == row + rel_ref[j]).astype(jnp.bfloat16)
        for side in range(2):
            part = jnp.dot(pick, kv_refs[j][side], preferred_element_type=jnp.float32)
            band[side] = part if band[side] is None else band[side] + part
    keys_b = band[0].astype(jnp.bfloat16)
    values_b = band[1].astype(jnp.bfloat16)
    squares = jnp.zeros((tok_count, DH), jnp.float32)
    for g in range(KV_HEADS):
        key = keys_b[:, g * DH : (g + 1) * DH]
        value = values_b[:, g * DH : (g + 1) * DH]
        heads = [slice(h * DH, (h + 1) * DH) for h in range(g * groups, (g + 1) * groups)]
        grouped = jnp.concatenate([q_ref[:, cols] for cols in heads], axis=0)
        scores = lax.dot_general(
            grouped, key, (((1,), (1,)), ((), ())), preferred_element_type=jnp.float32
        ) * (1.0 / math.sqrt(DH))
        weights = jnp.exp(scores - jnp.max(scores, axis=-1, keepdims=True))
        total = jnp.sum(weights, axis=-1, keepdims=True)
        context = jnp.dot(
            weights.astype(jnp.bfloat16), value, preferred_element_type=jnp.float32
        ) / total
        for i, cols in enumerate(heads):
            state = res_ref[:, cols].astype(jnp.float32) + context[i * tok_count : (i + 1) * tok_count]
            state_ref[:, cols] = state
            squares = squares + state * state
    squares = jnp.sum(squares, axis=-1, keepdims=True)
    scale = lax.rsqrt(squares / D + 1e-06)
    normed = (state_ref[...] * scale * gain_ref[...]).astype(jnp.bfloat16)
    for disp_ref, out_ref in zip(disp_refs, out_refs):
        out_ref[...] = jnp.dot(
            disp_ref[...], normed, preferred_element_type=jnp.float32
        ).astype(jnp.bfloat16)


def attend(rel, query_rows, residual, gain, shards, dispatch):
    tok_count = query_rows.shape[0]
    vmem = pl.BlockSpec(memory_space=pltpu.VMEM)
    outs = [jax.ShapeDtypeStruct((tok_count, D), jnp.float32)]
    outs += [jax.ShapeDtypeStruct((d.shape[0], D), jnp.bfloat16) for d in dispatch]
    return pl.pallas_call(
        functools.partial(attend_kernel, len(shards), len(dispatch)),
        out_shape=outs,
        in_specs=[pl.BlockSpec(memory_space=pltpu.SMEM)]
        + [vmem] * (3 + len(shards) + len(dispatch)),
        out_specs=[vmem] * len(outs),
        compiler_params=pltpu.CompilerParams(vmem_limit_bytes=VMEM_LIMIT),
        cost_estimate=pl.CostEstimate(
            flops=6 * tok_count * D * WIN, bytes_accessed=6_000_000, transcendentals=HEADS * WIN * tok_count
        ),
        name="attend",
    )(rel, query_rows, residual, gain, *shards, *dispatch)


def expert_kernel(count, *refs):
    x_refs = refs[:count]
    in_ref, out_w_ref = refs[count], refs[count + 1]
    out_refs = refs[count + 2 :]
    joined = all(ref.shape[0] % 8 == 0 for ref in x_refs)
    groups = [x_refs] if joined else [[ref] for ref in x_refs]
    targets = [out_refs] if joined else [[ref] for ref in out_refs]
    for sources, outs in zip(groups, targets):
        if len(sources) == 1:
            rows_b = sources[0][...]
        elif all(ref.shape[0] % 16 == 0 for ref in sources):
            rows_b = jnp.concatenate([ref[...] for ref in sources], axis=0)
        else:
            rows_b = [ref[...].astype(jnp.float32) for ref in sources]
            rows_b = jnp.concatenate(rows_b, axis=0).astype(jnp.bfloat16)
        hidden = lax.dot_general(
            rows_b, in_ref[...], (((1,), (1,)), ((), ())), preferred_element_type=jnp.float32
        )
        hidden = jnp.maximum(hidden, 0.0).astype(jnp.bfloat16)
        for at in range(0, D, SPAN):
            cols = slice(at, at + SPAN)
            part = jnp.dot(hidden, out_w_ref[:, cols], preferred_element_type=jnp.float32)
            begin = 0
            for out_ref in outs:
                rows = part[begin : begin + out_ref.shape[0]]
                out_ref[:, cols] = rows.astype(jnp.bfloat16)
                begin += out_ref.shape[0]


def pick_kernel(core_ref, in_ref, out_w_ref, pair_in_ref, pair_out_ref, sems):
    other = 1 - core_ref[0]
    copies = [
        pltpu.make_async_copy(in_ref.at[other], pair_in_ref, sems.at[0]),
        pltpu.make_async_copy(out_w_ref.at[other], pair_out_ref, sems.at[1]),
    ]
    for copy in copies:
        copy.start()
    for copy in copies:
        copy.wait()


def pool_kernel(core_ref, in_ref, out_w_ref, pair_in_ref, pair_out_ref, unit_in_ref, unit_out_ref, sems):
    core = core_ref[0]
    units = pair_in_ref.shape[0]
    copies = []
    sources = [
        (in_ref.at[core], pair_in_ref, unit_in_ref),
        (out_w_ref.at[core], pair_out_ref, unit_out_ref),
    ]
    for mine, other, target in sources:
        for at, source in enumerate((mine, other)):
            copies.append(
                pltpu.make_async_copy(
                    source, target.at[pl.ds(at * units, units)], sems.at[len(copies)]
                )
            )
    for copy in copies:
        copy.start()
    for copy in copies:
        copy.wait()


def staged(kernel, core, arrays, rows, copies, name):
    anywhere = pl.BlockSpec(memory_space=pl.ANY)
    vmem = pl.BlockSpec(memory_space=pltpu.VMEM)
    return pl.pallas_call(
        kernel,
        out_shape=[rows_like(rows), rows_like(rows)],
        in_specs=[pl.BlockSpec(memory_space=pltpu.SMEM)] + [anywhere] * len(arrays),
        out_specs=[vmem, vmem],
        scratch_shapes=[pltpu.SemaphoreType.DMA((copies,))],
        compiler_params=pltpu.CompilerParams(vmem_limit_bytes=EXPERT_VMEM),
        cost_estimate=pl.CostEstimate(
            flops=0, bytes_accessed=4 * rows * D * 2, transcendentals=0
        ),
        name=name,
    )(core, *arrays)


def expert_sums(parts, unit_in, unit_out):
    rows = [x.shape[0] for x in parts]
    units = unit_in.shape[0]
    vmem = pl.BlockSpec(memory_space=pltpu.VMEM)
    return pl.pallas_call(
        functools.partial(expert_kernel, len(parts)),
        out_shape=[jax.ShapeDtypeStruct((r, D), jnp.bfloat16) for r in rows],
        in_specs=[vmem] * (len(parts) + 2),
        out_specs=[vmem] * len(parts),
        compiler_params=pltpu.CompilerParams(vmem_limit_bytes=EXPERT_VMEM),
        cost_estimate=pl.CostEstimate(flops=1, bytes_accessed=1, transcendentals=0),
        name="expert",
    )(*parts, unit_in, unit_out)


def local(kernel, outs, *args, name):
    vmem = pl.BlockSpec(memory_space=pltpu.VMEM)
    moved = sum(x.size * x.dtype.itemsize for x in (*args, *outs))
    return pl.pallas_call(
        kernel,
        out_shape=outs,
        in_specs=[vmem] * len(args),
        out_specs=[vmem] * len(outs),
        compiler_params=pltpu.CompilerParams(vmem_limit_bytes=EXPERT_VMEM),
        cost_estimate=pl.CostEstimate(
            flops=moved // 2, bytes_accessed=moved, transcendentals=0
        ),
        name=name,
    )(*args)


def rows_like(rows):
    return jax.ShapeDtypeStruct((rows, D), jnp.bfloat16)


def join_slots(stayed, crossed):
    capacity = stayed[0].shape[0]
    if capacity % 8:
        return [
            jnp.concatenate([rows, crossed[i * capacity : (i + 1) * capacity]], axis=0)
            for i, rows in enumerate(stayed)
        ]

    def kernel(*refs):
        count = len(stayed)
        other = refs[count][...].astype(jnp.float32)
        for i in range(count):
            pair = [refs[i][...].astype(jnp.float32), other[i * capacity : (i + 1) * capacity]]
            refs[count + 1 + i][...] = jnp.concatenate(pair, axis=0).astype(jnp.bfloat16)

    outs = [rows_like(2 * capacity) for _ in stayed]
    return local(kernel, outs, *stayed, crossed, name="join_slots")


def split_rows(fore_rows, rear_rows, cut):
    size = fore_rows.shape[0]

    def kernel(fore_ref, rear_ref, *out_refs):
        out_refs = list(out_refs)
        if cut > 0:
            rows = fore_ref[...].astype(jnp.float32)[:cut]
            out_refs.pop(0)[...] = rows.astype(jnp.bfloat16)
        if cut < size:
            rows = rear_ref[...].astype(jnp.float32)[cut:]
            out_refs.pop(0)[...] = rows.astype(jnp.bfloat16)

    outs = [rows_like(rows) for rows in (cut, size - cut) if rows > 0]
    return local(kernel, outs, fore_rows, rear_rows, name="split_rows")


def add_sums(ahead_part, behind_part, ahead, behind, cut):
    size = ahead_part.shape[0]

    def filled(rows, before):
        rows = rows.astype(jnp.float32)
        edges = [jnp.zeros((before, D), jnp.float32)] if before else []
        edges.append(rows)
        after = size - before - rows.shape[0]
        if after:
            edges.append(jnp.zeros((after, D), jnp.float32))
        return jnp.concatenate(edges, axis=0) if len(edges) > 1 else rows

    totals = [x for x in (ahead, behind) if x is not None]

    def kernel(*refs):
        refs = list(refs)
        sums = [refs.pop(0)[...].astype(jnp.float32), refs.pop(0)[...].astype(jnp.float32)]
        if ahead is not None:
            sums[0] = sums[0] + filled(refs.pop(0)[...], 0)
        if behind is not None:
            sums[1] = sums[1] + filled(refs.pop(0)[...], size - behind.shape[0])
        for out_ref, total in zip(refs, sums):
            out_ref[...] = total.astype(jnp.bfloat16)

    outs = [rows_like(size), rows_like(size)]
    return local(kernel, outs, ahead_part, behind_part, *totals, name="add_sums")


def finish_sums(own, ahead, behind):
    def kernel(own_ref, ahead_ref, behind_ref, out_ref):
        total = own_ref[...].astype(jnp.float32) + ahead_ref[...].astype(jnp.float32)
        out_ref[...] = (total + behind_ref[...].astype(jnp.float32)).astype(jnp.bfloat16)

    return local(kernel, [rows_like(own.shape[0])], own, ahead, behind, name="finish_sums")[0]


def combine_kernel(blocks, state_ref, scale_ref, *refs):
    total = None
    for j in range(blocks):
        part = lax.dot_general(
            refs[j][...],
            refs[blocks + j][...],
            (((1,), (0,)), ((), ())),
            preferred_element_type=jnp.float32,
        )
        total = part if total is None else total + part
    refs[2 * blocks][...] = (state_ref[...] + scale_ref[...] * total).astype(jnp.bfloat16)


def combine(state, scale, undo, returned):
    tok_count = state.shape[0]
    blocks = len(undo)
    vmem = pl.BlockSpec(memory_space=pltpu.VMEM)
    return pl.pallas_call(
        functools.partial(combine_kernel, blocks),
        out_shape=jax.ShapeDtypeStruct((tok_count, D), jnp.bfloat16),
        in_specs=[vmem] * (2 + 2 * blocks),
        out_specs=vmem,
        compiler_params=pltpu.CompilerParams(vmem_limit_bytes=EXPERT_VMEM),
        cost_estimate=pl.CostEstimate(
            flops=2 * tok_count * tok_count * D, bytes_accessed=4_000_000, transcendentals=0
        ),
        name="combine",
    )(state, scale, *undo, *returned)


def body(
    queries, dec_state, enc_kv, band_start, norm_gain, route_ids, keep, route_prob, w_in, w_out
):
    sections = lax.axis_size("section")
    seqs = lax.axis_size("seq")
    depth = lax.axis_size("expert")
    chips = sections // CORES
    assert chips == 2 and w_in.shape[0] == CORES
    s = lax.axis_index("section")
    q = lax.axis_index("seq")
    core = s % CORES

    def route(source_of):
        pairs = []
        for a in range(sections):
            for b in range(seqs):
                origin = source_of(b)
                if origin is not None:
                    pairs.append((((a - 1) % sections) * seqs + origin, a * seqs + b))
        return pairs

    frames = enc_kv.shape[2]
    block = enc_kv[:, 0]
    if seqs == 2:
        shards = [
            lax.ppermute(block, ("section", "seq"), route(lambda b: b)),
            lax.ppermute(block, ("section", "seq"), route(lambda b: 1 - b)),
        ]
        origins = [q, 1 - q]
    else:
        shards = [
            lax.ppermute(block, ("section", "seq"), route(lambda b: b)),
            lax.ppermute(block, ("section", "seq"), route(lambda b: b - 1 if b > 0 else None)),
            lax.ppermute(
                block, ("section", "seq"), route(lambda b: b + 1 if b < seqs - 1 else None)
            ),
        ]
        origins = [q, q - 1, q + 1]
    rel = jnp.stack([band_start[0, 0] - origin * frames for origin in origins]).astype(jnp.int32)

    def core_pairs():
        return [(a, a ^ 1) for a in range(sections)]

    core_at = core.astype(jnp.int32)[None]
    share = w_in.shape[1]
    pair_units = staged(pick_kernel, core_at, [w_in, w_out], share, 2, "pick_units")
    rel, pair_units = lax.optimization_barrier((rel, pair_units))
    pair_units = [lax.ppermute(rows, "section", core_pairs()) for rows in pair_units]

    experts_of = route_ids[0, :, 0]
    tok_count = experts_of.shape[0]
    expert_count = seqs * CORES
    capacity = max(2, tok_count // expert_count)
    one_hot = (experts_of[:, None] == jnp.arange(expert_count, dtype=jnp.int32)[None, :]).astype(
        jnp.int32
    )
    slot_of = jnp.sum((jnp.cumsum(one_hot, axis=0) - one_hot) * one_hot, axis=1)
    kept = keep[0] == 1
    turns = [(dq, dc) for dq in range(seqs) for dc in range(CORES)]
    slots = jnp.arange(capacity, dtype=jnp.int32)
    dispatch, undo = [], []
    block_slots = jnp.arange(CORES * capacity, dtype=jnp.int32)
    for dq, dc in turns:
        named = ((q + dq) % seqs) * CORES + (core ^ dc)
        code = jnp.where(kept & (experts_of == named), slot_of, -1)
        dispatch.append((slots[:, None] == code[None, :]).astype(jnp.bfloat16))
        code = jnp.where(code >= 0, code + dc * capacity, -1)
        undo.append((code[:, None] == block_slots[None, :]).astype(jnp.bfloat16))
    scale = (keep[0].astype(jnp.float32) * route_prob[0])[:, None]

    crossing = jnp.concatenate(
        [rows for (dq, dc), rows in zip(turns, dispatch) if dc == 1], axis=0
    )
    staying = [rows for (dq, dc), rows in zip(turns, dispatch) if dc == 0]
    rel, crossing, staying, undo, scale = lax.optimization_barrier(
        (rel, crossing, staying, undo, scale)
    )
    state, crossed, *stayed = attend(
        rel, queries[0], dec_state[0], norm_gain[None, :], shards, [crossing] + staying
    )

    def core_swap(rows):
        return lax.ppermute(rows, "section", core_pairs())

    def seq_move(rows, step):
        return lax.ppermute(rows, "seq", [(b, (b + step) % seqs) for b in range(seqs)])

    slot_blocks = join_slots(stayed, core_swap(crossed))
    moved = [seq_move(slot_blocks[dq], dq) for dq in range(1, seqs)]
    parts = [slot_blocks[0], moved[0] if seqs == 2 else jnp.concatenate(moved, axis=0)]

    unit_in, unit_out = staged(
        pool_kernel, core_at, [w_in, w_out, *pair_units], CORES * share, 4, "pool_units"
    )
    parts[1], unit_in, unit_out = lax.optimization_barrier((parts[1], unit_in, unit_out))

    cycle = [(0, z) for z in range(depth)] + [(1, z) for z in reversed(range(depth))]
    count = len(cycle)

    def hop(rows, step):
        pairs = []
        for c in range(CORES):
            ids = [(x * CORES + c) * depth + z for x, z in cycle]
            pairs += [(ids[i], ids[(i + step) % count]) for i in range(count)]
        return lax.ppermute(rows, ("section", "expert"), pairs)

    half = count // 2
    sizes = [rows.shape[0] for rows in parts]
    cut = [
        rows // 2 if rows // 2 % 8 == 0 else rows * (1 - p) for p, rows in enumerate(sizes)
    ]
    fore = [[rows] for rows in parts]
    rear = [[rows] for rows in parts]
    sums = {}

    def after(keys, rows):
        for key in keys:
            if key in sums:
                rows, sums[key] = lax.optimization_barrier((rows, sums[key]))
        return rows

    for k in range(1, half):
        for p in range(2):
            rows = lax.optimization_barrier((fore[p][-1], rear[p][-1]))
            if p == 1:
                rows = after([(0, k - 1), (1, k - 2)], rows)
            fore[p].append(hop(rows[0], 1))
            rear[p].append(hop(rows[1], -1))
            if k < half - 1:
                sums[p, k] = expert_sums([fore[p][k], rear[p][k]], unit_in, unit_out)
    rows = (fore[0][-1], rear[0][-1])
    lead = split_rows(*rows, cut[0])
    rows, lead = lax.optimization_barrier((rows, lead))
    sums[0, half - 1] = expert_sums(rows, unit_in, unit_out)
    rows = (fore[1][-1], rear[1][-1])
    follow = split_rows(*after([(0, half - 1), (1, half - 2)], rows), cut[1])
    rows, follow = lax.optimization_barrier((rows, follow))
    sums[1, half - 1] = expert_sums(rows, unit_in, unit_out)
    ahead_part, behind_part = [{}, {}], [{}, {}]
    for p, rows in enumerate((lead, follow)):
        got = []
        if cut[p] > 0:
            got.append(hop(rows[0], 1))
        if cut[p] < sizes[p]:
            got.append(hop(rows[-1], -1))
        if p == 0:
            got = after([(1, half - 1)], got)
        sums[p, half] = expert_sums(got, unit_in, unit_out)
    for p, k in list(sums):
        got = list(sums[p, k])
        if k < half:
            behind_part[p][k], ahead_part[p][k] = got
            continue
        if cut[p] > 0:
            ahead_part[p][half] = got.pop(0)
        if cut[p] < sizes[p]:
            behind_part[p][half] = got.pop(0)

    ahead, behind = [None, None], [None, None]
    for p in range(2):
        if half in ahead_part[p]:
            ahead[p] = hop(ahead_part[p][half], 1)
        if half in behind_part[p]:
            behind[p] = hop(behind_part[p][half], -1)
    (ahead[0], behind[0]), parts = lax.optimization_barrier(((ahead[0], behind[0]), parts))
    own = expert_sums(parts, unit_in, unit_out)
    for k in range(half - 1, 0, -1):
        for p in (1, 0):
            totals = add_sums(
                ahead_part[p][k], behind_part[p][k], ahead[p], behind[p], cut[p]
            )
            if k == 1 and p == 1:
                totals, own = lax.optimization_barrier((totals, own))
            ahead[p], behind[p] = hop(totals[0], 1), hop(totals[1], -1)
    done = [finish_sums(own[p], ahead[p], behind[p]) for p in range(2)]

    width = CORES * capacity
    if seqs == 2:
        far = [done[1]]
    else:
        far = [done[1][i * width : (i + 1) * width] for i in range(seqs - 1)]
    returned = []
    for dq, rows in enumerate([done[0]] + far):
        rows = seq_move(rows, -dq) if dq else rows
        returned += [rows, core_swap(rows)]
    return combine(state, scale, undo, returned)[None]


def solution(mesh):
    return jax.shard_map(
        body,
        mesh=mesh,
        in_specs=(
            P(("section", "expert"), "seq", None),
            P(("section", "expert"), "seq", None),
            P(None, ("section", "expert"), "seq", None),
            P(("section", "expert"), "seq"),
            P(),
            P(("section", "expert"), "seq", None),
            P(("section", "expert"), "seq"),
            P(("section", "expert"), "seq"),
            P("seq", ("section", "expert"), None),
            P("seq", ("section", "expert"), None),
        ),
        out_specs=P(("section", "expert"), "seq", None),
        check_vma=False,
    )
```

```python
import functools
import math

import jax
import jax.numpy as jnp
from jax import lax
from jax.experimental import pallas as pl
from jax.experimental.pallas import tpu as pltpu
from jax.sharding import PartitionSpec as P

D = 4096
HEADS = 32
KV_HEADS = 8
DH = 128
WIN = 128
CORES = 2
VMEM_LIMIT = 16 * 1024 * 1024
EXPERT_VMEM = 8 * 1024 * 1024
SPAN = 1024


def attend_kernel(shards, blocks, rel_ref, q_ref, res_ref, gain_ref, *refs):
    kv_refs = refs[:shards]
    disp_refs = refs[shards : shards + blocks]
    state_ref = refs[shards + blocks]
    out_refs = refs[shards + blocks + 1 :]
    tok_count = q_ref.shape[0]
    groups = HEADS // KV_HEADS
    frames = kv_refs[0].shape[1]
    row = lax.broadcasted_iota(jnp.int32, (WIN, frames), 0)
    col = lax.broadcasted_iota(jnp.int32, (WIN, frames), 1)
    band = [None, None]
    for j in range(shards):
        pick = (col == row + rel_ref[j]).astype(jnp.bfloat16)
        for side in range(2):
            part = jnp.dot(pick, kv_refs[j][side], preferred_element_type=jnp.float32)
            band[side] = part if band[side] is None else band[side] + part
    keys_b = band[0].astype(jnp.bfloat16)
    values_b = band[1].astype(jnp.bfloat16)
    squares = jnp.zeros((tok_count, DH), jnp.float32)
    for g in range(KV_HEADS):
        key = keys_b[:, g * DH : (g + 1) * DH]
        value = values_b[:, g * DH : (g + 1) * DH]
        heads = [slice(h * DH, (h + 1) * DH) for h in range(g * groups, (g + 1) * groups)]
        grouped = jnp.concatenate([q_ref[:, cols] for cols in heads], axis=0)
        scores = lax.dot_general(
            grouped, key, (((1,), (1,)), ((), ())), preferred_element_type=jnp.float32
        ) * (1.0 / math.sqrt(DH))
        weights = jnp.exp(scores - jnp.max(scores, axis=-1, keepdims=True))
        total = jnp.sum(weights, axis=-1, keepdims=True)
        context = jnp.dot(
            weights.astype(jnp.bfloat16), value, preferred_element_type=jnp.float32
        ) / total
        for i, cols in enumerate(heads):
            state = res_ref[:, cols].astype(jnp.float32) + context[i * tok_count : (i + 1) * tok_count]
            state_ref[:, cols] = state
            squares = squares + state * state
    squares = jnp.sum(squares, axis=-1, keepdims=True)
    scale = lax.rsqrt(squares / D + 1e-06)
    normed = (state_ref[...] * scale * gain_ref[...]).astype(jnp.bfloat16)
    for disp_ref, out_ref in zip(disp_refs, out_refs):
        out_ref[...] = jnp.dot(
            disp_ref[...], normed, preferred_element_type=jnp.float32
        ).astype(jnp.bfloat16)


def attend(rel, query_rows, residual, gain, shards, dispatch):
    tok_count = query_rows.shape[0]
    vmem = pl.BlockSpec(memory_space=pltpu.VMEM)
    outs = [jax.ShapeDtypeStruct((tok_count, D), jnp.float32)]
    outs += [jax.ShapeDtypeStruct((d.shape[0], D), jnp.bfloat16) for d in dispatch]
    return pl.pallas_call(
        functools.partial(attend_kernel, len(shards), len(dispatch)),
        out_shape=outs,
        in_specs=[pl.BlockSpec(memory_space=pltpu.SMEM)]
        + [vmem] * (3 + len(shards) + len(dispatch)),
        out_specs=[vmem] * len(outs),
        compiler_params=pltpu.CompilerParams(vmem_limit_bytes=VMEM_LIMIT),
        cost_estimate=pl.CostEstimate(
            flops=6 * tok_count * D * WIN, bytes_accessed=6_000_000, transcendentals=HEADS * WIN * tok_count
        ),
        name="attend",
    )(rel, query_rows, residual, gain, *shards, *dispatch)


def expert_kernel(count, *refs):
    x_refs = refs[:count]
    in_ref, out_w_ref = refs[count], refs[count + 1]
    out_refs = refs[count + 2 :]
    joined = all(ref.shape[0] % 8 == 0 for ref in x_refs)
    groups = [x_refs] if joined else [[ref] for ref in x_refs]
    targets = [out_refs] if joined else [[ref] for ref in out_refs]
    for sources, outs in zip(groups, targets):
        if len(sources) == 1:
            rows_b = sources[0][...]
        elif all(ref.shape[0] % 16 == 0 for ref in sources):
            rows_b = jnp.concatenate([ref[...] for ref in sources], axis=0)
        else:
            rows_b = [ref[...].astype(jnp.float32) for ref in sources]
            rows_b = jnp.concatenate(rows_b, axis=0).astype(jnp.bfloat16)
        hidden = lax.dot_general(
            rows_b, in_ref[...], (((1,), (1,)), ((), ())), preferred_element_type=jnp.float32
        )
        hidden = jnp.maximum(hidden, 0.0).astype(jnp.bfloat16)
        for at in range(0, D, SPAN):
            cols = slice(at, at + SPAN)
            part = jnp.dot(hidden, out_w_ref[:, cols], preferred_element_type=jnp.float32)
            begin = 0
            for out_ref in outs:
                rows = part[begin : begin + out_ref.shape[0]]
                out_ref[:, cols] = rows.astype(jnp.bfloat16)
                begin += out_ref.shape[0]


def pick_kernel(core_ref, in_ref, out_w_ref, pair_in_ref, pair_out_ref, sems):
    other = 1 - core_ref[0]
    copies = [
        pltpu.make_async_copy(in_ref.at[other], pair_in_ref, sems.at[0]),
        pltpu.make_async_copy(out_w_ref.at[other], pair_out_ref, sems.at[1]),
    ]
    for copy in copies:
        copy.start()
    for copy in copies:
        copy.wait()


def stage_kernel(core_ref, q_ref, res_ref, q_out_ref, res_out_ref, sems):
    copies = [
        pltpu.make_async_copy(q_ref, q_out_ref, sems.at[0]),
        pltpu.make_async_copy(res_ref, res_out_ref, sems.at[1]),
    ]
    for copy in copies:
        copy.start()
    for copy in copies:
        copy.wait()


def pool_kernel(core_ref, in_ref, out_w_ref, pair_in_ref, pair_out_ref, unit_in_ref, unit_out_ref, sems):
    core = core_ref[0]
    units = pair_in_ref.shape[0]
    copies = []
    sources = [
        (in_ref.at[core], pair_in_ref, unit_in_ref),
        (out_w_ref.at[core], pair_out_ref, unit_out_ref),
    ]
    for mine, other, target in sources:
        for at, source in enumerate((mine, other)):
            copies.append(
                pltpu.make_async_copy(
                    source, target.at[pl.ds(at * units, units)], sems.at[len(copies)]
                )
            )
    for copy in copies:
        copy.start()
    for copy in copies:
        copy.wait()


def staged(kernel, core, arrays, outs, copies, name):
    vmem = pl.BlockSpec(memory_space=pltpu.VMEM)
    return pl.pallas_call(
        kernel,
        out_shape=outs,
        in_specs=[pl.BlockSpec(memory_space=pltpu.SMEM)]
        + [pl.BlockSpec(memory_space=pl.ANY)] * len(arrays),
        out_specs=[vmem] * len(outs),
        scratch_shapes=[pltpu.SemaphoreType.DMA((copies,))],
        compiler_params=pltpu.CompilerParams(vmem_limit_bytes=EXPERT_VMEM),
        cost_estimate=pl.CostEstimate(
            flops=0, bytes_accessed=sum(2 * x.size * 2 for x in outs), transcendentals=0
        ),
        name=name,
    )(core, *arrays)


def expert_sums(parts, unit_in, unit_out):
    rows = [x.shape[0] for x in parts]
    units = unit_in.shape[0]
    vmem = pl.BlockSpec(memory_space=pltpu.VMEM)
    return pl.pallas_call(
        functools.partial(expert_kernel, len(parts)),
        out_shape=[jax.ShapeDtypeStruct((r, D), jnp.bfloat16) for r in rows],
        in_specs=[vmem] * (len(parts) + 2),
        out_specs=[vmem] * len(parts),
        compiler_params=pltpu.CompilerParams(vmem_limit_bytes=EXPERT_VMEM),
        cost_estimate=pl.CostEstimate(flops=1, bytes_accessed=1, transcendentals=0),
        name="expert",
    )(*parts, unit_in, unit_out)


def local(kernel, outs, *args, name):
    vmem = pl.BlockSpec(memory_space=pltpu.VMEM)
    moved = sum(x.size * x.dtype.itemsize for x in (*args, *outs))
    return pl.pallas_call(
        kernel,
        out_shape=outs,
        in_specs=[vmem] * len(args),
        out_specs=[vmem] * len(outs),
        compiler_params=pltpu.CompilerParams(vmem_limit_bytes=EXPERT_VMEM),
        cost_estimate=pl.CostEstimate(
            flops=moved // 2, bytes_accessed=moved, transcendentals=0
        ),
        name=name,
    )(*args)


def rows_like(rows):
    return jax.ShapeDtypeStruct((rows, D), jnp.bfloat16)


def join_slots(stayed, crossed):
    capacity = stayed[0].shape[0]
    if capacity % 8:
        return [
            jnp.concatenate([rows, crossed[i * capacity : (i + 1) * capacity]], axis=0)
            for i, rows in enumerate(stayed)
        ]

    def kernel(*refs):
        count = len(stayed)
        other = refs[count][...].astype(jnp.float32)
        for i in range(count):
            pair = [refs[i][...].astype(jnp.float32), other[i * capacity : (i + 1) * capacity]]
            refs[count + 1 + i][...] = jnp.concatenate(pair, axis=0).astype(jnp.bfloat16)

    outs = [rows_like(2 * capacity) for _ in stayed]
    return local(kernel, outs, *stayed, crossed, name="join_slots")


def add_sums(parts, totals):
    def kernel(*refs):
        for part_ref, total_ref, out_ref in zip(refs[:2], refs[2:4], refs[4:]):
            total = part_ref[...].astype(jnp.float32) + total_ref[...].astype(jnp.float32)
            out_ref[...] = total.astype(jnp.bfloat16)

    return local(kernel, [rows_like(x.shape[0]) for x in parts], *parts, *totals, name="add_sums")


def finish_sums(*terms, pieces=1):
    size = terms[0].shape[0] // pieces

    def kernel(*refs):
        total = refs[0][...].astype(jnp.float32)
        for ref in refs[1 : len(terms)]:
            total = total + ref[...].astype(jnp.float32)
        for i, out_ref in enumerate(refs[len(terms) :]):
            out_ref[...] = total[i * size : (i + 1) * size].astype(jnp.bfloat16)

    return local(kernel, [rows_like(size)] * pieces, *terms, name="finish_sums")


def combine_kernel(blocks, state_ref, scale_ref, undo_ref, *refs):
    if refs[0].shape[0] % 8 == 0:
        rows = [ref[...].astype(jnp.float32) for ref in refs[:blocks]]
        rows = [jnp.concatenate(rows, axis=0).astype(jnp.bfloat16)]
    else:
        rows = [ref[...] for ref in refs[:blocks]]
    begin, total = 0, None
    for part in rows:
        pick = undo_ref[:, begin : begin + part.shape[0]]
        begin += part.shape[0]
        part = jnp.dot(pick, part, preferred_element_type=jnp.float32)
        total = part if total is None else total + part
    refs[blocks][...] = (state_ref[...] + scale_ref[...] * total).astype(jnp.bfloat16)


def combine(state, scale, undo, returned):
    tok_count = state.shape[0]
    blocks = len(returned)
    vmem = pl.BlockSpec(memory_space=pltpu.VMEM)
    return pl.pallas_call(
        functools.partial(combine_kernel, blocks),
        out_shape=jax.ShapeDtypeStruct((tok_count, D), jnp.bfloat16),
        in_specs=[vmem] * (3 + blocks),
        out_specs=vmem,
        compiler_params=pltpu.CompilerParams(vmem_limit_bytes=EXPERT_VMEM),
        cost_estimate=pl.CostEstimate(
            flops=2 * tok_count * tok_count * D, bytes_accessed=4_000_000, transcendentals=0
        ),
        name="combine",
    )(state, scale, undo, *returned)


def body(
    queries, dec_state, enc_kv, band_start, norm_gain, route_ids, keep, route_prob, w_in, w_out
):
    sections = lax.axis_size("section")
    seqs = lax.axis_size("seq")
    depth = lax.axis_size("expert")
    chips = sections // CORES
    assert chips == 2 and w_in.shape[0] == CORES
    s = lax.axis_index("section")
    q = lax.axis_index("seq")
    core = s % CORES

    def route(source_of):
        pairs = []
        for a in range(sections):
            for b in range(seqs):
                origin = source_of(b)
                if origin is not None:
                    pairs.append((((a - 1) % sections) * seqs + origin, a * seqs + b))
        return pairs

    frames = enc_kv.shape[2]
    block = enc_kv[:, 0]
    if seqs == 2:
        shards = [
            lax.ppermute(block, ("section", "seq"), route(lambda b: 1 - b)),
            lax.ppermute(block, ("section", "seq"), route(lambda b: b)),
        ]
        origins = [1 - q, q]
    else:
        shards = [
            lax.ppermute(block, ("section", "seq"), route(lambda b: b)),
            lax.ppermute(block, ("section", "seq"), route(lambda b: b - 1 if b > 0 else None)),
            lax.ppermute(
                block, ("section", "seq"), route(lambda b: b + 1 if b < seqs - 1 else None)
            ),
        ]
        origins = [q, q - 1, q + 1]
    rel = jnp.stack([band_start[0, 0] - origin * frames for origin in origins]).astype(jnp.int32)

    def core_pairs():
        return [(a, a ^ 1) for a in range(sections)]

    core_at = core.astype(jnp.int32)[None]
    share = w_in.shape[1]
    pair_units = staged(
        pick_kernel, core_at, [w_in, w_out], [rows_like(share)] * 2, 2, "pick_units"
    )
    rel, pair_units = lax.optimization_barrier((rel, pair_units))
    pair_units = [lax.ppermute(rows, "section", core_pairs()) for rows in pair_units]

    experts_of = route_ids[0, :, 0]
    tok_count = experts_of.shape[0]
    expert_count = seqs * CORES
    capacity = max(2, tok_count // expert_count)
    one_hot = (experts_of[:, None] == jnp.arange(expert_count, dtype=jnp.int32)[None, :]).astype(
        jnp.int32
    )
    slot_of = jnp.sum((jnp.cumsum(one_hot, axis=0) - one_hot) * one_hot, axis=1)
    kept = keep[0] == 1
    turns = [(dq, dc) for dq in range(seqs) for dc in range(CORES)]
    slots = jnp.arange(capacity, dtype=jnp.int32)
    dispatch, undo = [], []
    for dq, dc in turns:
        named = ((q + dq) % seqs) * CORES + (core ^ dc)
        code = jnp.where(kept & (experts_of == named), slot_of, -1)
        dispatch.append((slots[:, None] == code[None, :]).astype(jnp.bfloat16))
        undo.append((code[:, None] == slots[None, :]).astype(jnp.bfloat16))
    undo = jnp.concatenate(undo, axis=1)
    scale = (keep[0].astype(jnp.float32) * route_prob[0])[:, None]

    crossing = jnp.concatenate(
        [rows for (dq, dc), rows in zip(turns, dispatch) if dc == 1], axis=0
    )
    staying = [rows for (dq, dc), rows in zip(turns, dispatch) if dc == 0]
    ready, rel, crossing, staying, undo, scale = lax.optimization_barrier(
        (core_at, rel, crossing, staying, undo, scale)
    )
    query_rows, residual = staged(
        stage_kernel,
        ready,
        [queries[0], dec_state[0]],
        [rows_like(tok_count)] * 2,
        2,
        "stage_rows",
    )
    state, crossed, *stayed = attend(
        rel, query_rows, residual, norm_gain[None, :], shards, [crossing] + staying
    )

    def core_swap(rows):
        return lax.ppermute(rows, "section", core_pairs())

    def seq_move(rows, step):
        return lax.ppermute(rows, "seq", [(b, (b + step) % seqs) for b in range(seqs)])

    slot_blocks = join_slots(stayed, core_swap(crossed))
    moved = [seq_move(slot_blocks[dq], dq) for dq in range(1, seqs)]
    parts = [slot_blocks[0], moved[0] if seqs == 2 else jnp.concatenate(moved, axis=0)]

    unit_in, unit_out = staged(
        pool_kernel,
        core_at,
        [w_in, w_out, *pair_units],
        [rows_like(CORES * share)] * 2,
        4,
        "pool_units",
    )
    parts[1], unit_in, unit_out = lax.optimization_barrier((parts[1], unit_in, unit_out))

    cycle = [(0, z) for z in range(depth)] + [(1, z) for z in reversed(range(depth))]
    count = len(cycle)

    def hop(rows, step):
        pairs = []
        for c in range(CORES):
            ids = [(x * CORES + c) * depth + z for x, z in cycle]
            pairs += [(ids[i], ids[(i + step) % count]) for i in range(count)]
        return lax.ppermute(rows, ("section", "expert"), pairs)

    half = count // 2
    fore = [[rows] for rows in parts]
    rear = [[rows] for rows in parts]
    sums = {}

    def after(keys, rows):
        for key in keys:
            if key in sums:
                rows, sums[key] = lax.optimization_barrier((rows, sums[key]))
        return rows

    for k in range(1, half):
        for p in range(2):
            rows = lax.optimization_barrier((fore[p][-1], rear[p][-1]))
            if p == 1:
                rows = after([(0, k - 1), (1, k - 2)], rows)
            fore[p].append(hop(rows[0], 1))
            rear[p].append(hop(rows[1], -1))
            if k < half - 1:
                sums[p, k] = expert_sums([fore[p][k], rear[p][k]], unit_in, unit_out)
    fore[0].append(hop(fore[0][-1], 1))
    rear[1].append(hop(rear[1][-1], -1))
    ahead_part, behind_part = [{}, {}], [{}, {}]
    for (p, k), got in sums.items():
        behind_part[p][k], ahead_part[p][k] = got
    k = half - 1
    behind_part[0][k], ahead_part[1][k] = expert_sums(
        [fore[0][k], rear[1][k]], unit_in, unit_out
    )
    ahead_part[0][k], behind_part[1][k] = expert_sums(
        [rear[0][k], fore[1][k]], unit_in, unit_out
    )
    lead = [behind_part[0][k], ahead_part[1][k]]
    fore[0][half], lead = lax.optimization_barrier((fore[0][half], lead))
    behind_part[0][k], ahead_part[1][k] = lead
    ahead_part[0][half] = expert_sums([fore[0][half]], unit_in, unit_out)[0]
    behind_part[1][half] = expert_sums([rear[1][half]], unit_in, unit_out)[0]

    short = [hop(behind_part[0][half - 1], -1), hop(ahead_part[1][half - 1], 1)]
    long = [hop(ahead_part[0][half], 1), hop(behind_part[1][half], -1)]
    (short, parts) = lax.optimization_barrier((short, parts))
    own = expert_sums(parts, unit_in, unit_out)
    for k in range(half - 1, 0, -1):
        if k < half - 1:
            totals = add_sums([behind_part[0][k], ahead_part[1][k]], short)
            if k == 1:
                totals, own = lax.optimization_barrier((totals, own))
            short = [hop(totals[0], -1), hop(totals[1], 1)]
        totals = add_sums([ahead_part[0][k], behind_part[1][k]], long)
        long = [hop(totals[0], 1), hop(totals[1], -1)]
    def cross(rows, dq, dc):
        pairs = [
            ((a ^ dc) * seqs + (b + dq) % seqs, a * seqs + b)
            for a in range(sections)
            for b in range(seqs)
        ]
        return lax.ppermute(rows, ("section", "seq"), pairs)

    if seqs == 2 and capacity % 8 == 0:
        blocks = finish_sums(own[1], short[1], long[1], pieces=CORES)
        blocks = [*finish_sums(own[0], short[0], long[0], pieces=CORES), *blocks]
    else:
        near = finish_sums(own[0], short[0], long[0])[0]
        far = finish_sums(own[1], short[1], long[1])[0]
        blocks = [near[i * capacity : (i + 1) * capacity] for i in range(CORES)]
        blocks += [far[i * capacity : (i + 1) * capacity] for i in range(len(turns) - CORES)]
    returned = [
        cross(rows, dq, dc) if dq or dc else rows for (dq, dc), rows in zip(turns, blocks)
    ]
    return combine(state, scale, undo, returned)[None]


def solution(mesh):
    return jax.shard_map(
        body,
        mesh=mesh,
        in_specs=(
            P(("section", "expert"), "seq", None),
            P(("section", "expert"), "seq", None),
            P(None, ("section", "expert"), "seq", None),
            P(("section", "expert"), "seq"),
            P(),
            P(("section", "expert"), "seq", None),
            P(("section", "expert"), "seq"),
            P(("section", "expert"), "seq"),
            P("seq", ("section", "expert"), None),
            P("seq", ("section", "expert"), None),
        ),
        out_specs=P(("section", "expert"), "seq", None),
        check_vma=False,
    )
```

```python
import functools
import math

import jax
import jax.numpy as jnp
from jax import lax
from jax.experimental import pallas as pl
from jax.experimental.pallas import tpu as pltpu
from jax.sharding import PartitionSpec as P

D = 4096
HEADS = 32
KV_HEADS = 8
DH = 128
WIN = 128
CORES = 2
VMEM_LIMIT = 16 * 1024 * 1024
EXPERT_VMEM = 8 * 1024 * 1024
SPAN = 1024


def attend_kernel(shards, blocks, rel_ref, q_ref, res_ref, gain_ref, *refs):
    kv_refs = refs[:shards]
    disp_refs = refs[shards : shards + blocks]
    state_ref = refs[shards + blocks]
    out_refs = refs[shards + blocks + 1 :]
    tok_count = q_ref.shape[0]
    groups = HEADS // KV_HEADS
    frames = kv_refs[0].shape[1]
    row = lax.broadcasted_iota(jnp.int32, (WIN, frames), 0)
    col = lax.broadcasted_iota(jnp.int32, (WIN, frames), 1)
    band = [None, None]
    for j in range(shards):
        pick = (col == row + rel_ref[j]).astype(jnp.bfloat16)
        for side in range(2):
            part = jnp.dot(pick, kv_refs[j][side], preferred_element_type=jnp.float32)
            band[side] = part if band[side] is None else band[side] + part
    keys_b = band[0].astype(jnp.bfloat16)
    values_b = band[1].astype(jnp.bfloat16)
    squares = jnp.zeros((tok_count, DH), jnp.float32)
    for g in range(KV_HEADS):
        key = keys_b[:, g * DH : (g + 1) * DH]
        value = values_b[:, g * DH : (g + 1) * DH]
        heads = [slice(h * DH, (h + 1) * DH) for h in range(g * groups, (g + 1) * groups)]
        grouped = jnp.concatenate([q_ref[:, cols] for cols in heads], axis=0)
        scores = lax.dot_general(
            grouped, key, (((1,), (1,)), ((), ())), preferred_element_type=jnp.float32
        ) * (1.0 / math.sqrt(DH))
        weights = jnp.exp(scores - jnp.max(scores, axis=-1, keepdims=True))
        total = jnp.sum(weights, axis=-1, keepdims=True)
        context = jnp.dot(
            weights.astype(jnp.bfloat16), value, preferred_element_type=jnp.float32
        ) / total
        for i, cols in enumerate(heads):
            state = res_ref[:, cols].astype(jnp.float32) + context[i * tok_count : (i + 1) * tok_count]
            state_ref[:, cols] = state
            squares = squares + state * state
    squares = jnp.sum(squares, axis=-1, keepdims=True)
    scale = lax.rsqrt(squares / D + 1e-06)
    normed = (state_ref[...] * scale * gain_ref[...]).astype(jnp.bfloat16)
    for disp_ref, out_ref in zip(disp_refs, out_refs):
        out_ref[...] = jnp.dot(
            disp_ref[...], normed, preferred_element_type=jnp.float32
        ).astype(jnp.bfloat16)


def attend(rel, query_rows, residual, gain, shards, dispatch):
    tok_count = query_rows.shape[0]
    vmem = pl.BlockSpec(memory_space=pltpu.VMEM)
    outs = [jax.ShapeDtypeStruct((tok_count, D), jnp.float32)]
    outs += [jax.ShapeDtypeStruct((d.shape[0], D), jnp.bfloat16) for d in dispatch]
    return pl.pallas_call(
        functools.partial(attend_kernel, len(shards), len(dispatch)),
        out_shape=outs,
        in_specs=[pl.BlockSpec(memory_space=pltpu.SMEM)]
        + [vmem] * (3 + len(shards) + len(dispatch)),
        out_specs=[vmem] * len(outs),
        compiler_params=pltpu.CompilerParams(vmem_limit_bytes=VMEM_LIMIT),
        cost_estimate=pl.CostEstimate(
            flops=6 * tok_count * D * WIN, bytes_accessed=6_000_000, transcendentals=HEADS * WIN * tok_count
        ),
        name="attend",
    )(rel, query_rows, residual, gain, *shards, *dispatch)


def expert_kernel(count, *refs):
    x_refs = refs[:count]
    in_ref, out_w_ref = refs[count], refs[count + 1]
    out_refs = refs[count + 2 :]
    joined = all(ref.shape[0] % 8 == 0 for ref in x_refs)
    groups = [x_refs] if joined else [[ref] for ref in x_refs]
    targets = [out_refs] if joined else [[ref] for ref in out_refs]
    for sources, outs in zip(groups, targets):
        if len(sources) == 1:
            rows_b = sources[0][...]
        elif all(ref.shape[0] % 16 == 0 for ref in sources):
            rows_b = jnp.concatenate([ref[...] for ref in sources], axis=0)
        else:
            rows_b = [ref[...].astype(jnp.float32) for ref in sources]
            rows_b = jnp.concatenate(rows_b, axis=0).astype(jnp.bfloat16)
        hidden = lax.dot_general(
            rows_b, in_ref[...], (((1,), (1,)), ((), ())), preferred_element_type=jnp.float32
        )
        hidden = jnp.maximum(hidden, 0.0).astype(jnp.bfloat16)
        for at in range(0, D, SPAN):
            cols = slice(at, at + SPAN)
            part = jnp.dot(hidden, out_w_ref[:, cols], preferred_element_type=jnp.float32)
            begin = 0
            for out_ref in outs:
                rows = part[begin : begin + out_ref.shape[0]]
                out_ref[:, cols] = rows.astype(jnp.bfloat16)
                begin += out_ref.shape[0]


def pick_kernel(core_ref, in_ref, out_w_ref, pair_in_ref, pair_out_ref, sems):
    other = 1 - core_ref[0]
    copies = [
        pltpu.make_async_copy(in_ref.at[other], pair_in_ref, sems.at[0]),
        pltpu.make_async_copy(out_w_ref.at[other], pair_out_ref, sems.at[1]),
    ]
    for copy in copies:
        copy.start()
    for copy in copies:
        copy.wait()


def stage_kernel(core_ref, q_ref, res_ref, q_out_ref, res_out_ref, sems):
    copies = [
        pltpu.make_async_copy(q_ref, q_out_ref, sems.at[0]),
        pltpu.make_async_copy(res_ref, res_out_ref, sems.at[1]),
    ]
    for copy in copies:
        copy.start()
    for copy in copies:
        copy.wait()


def pool_kernel(core_ref, in_ref, out_w_ref, pair_in_ref, pair_out_ref, unit_in_ref, unit_out_ref, sems):
    core = core_ref[0]
    units = pair_in_ref.shape[0]
    copies = []
    sources = [
        (in_ref.at[core], pair_in_ref, unit_in_ref),
        (out_w_ref.at[core], pair_out_ref, unit_out_ref),
    ]
    for mine, other, target in sources:
        for at, source in enumerate((mine, other)):
            copies.append(
                pltpu.make_async_copy(
                    source, target.at[pl.ds(at * units, units)], sems.at[len(copies)]
                )
            )
    for copy in copies:
        copy.start()
    for copy in copies:
        copy.wait()


def staged(kernel, core, arrays, outs, copies, name):
    vmem = pl.BlockSpec(memory_space=pltpu.VMEM)
    return pl.pallas_call(
        kernel,
        out_shape=outs,
        in_specs=[pl.BlockSpec(memory_space=pltpu.SMEM)]
        + [pl.BlockSpec(memory_space=pl.ANY)] * len(arrays),
        out_specs=[vmem] * len(outs),
        scratch_shapes=[pltpu.SemaphoreType.DMA((copies,))],
        compiler_params=pltpu.CompilerParams(vmem_limit_bytes=EXPERT_VMEM),
        cost_estimate=pl.CostEstimate(
            flops=0, bytes_accessed=sum(2 * x.size * 2 for x in outs), transcendentals=0
        ),
        name=name,
    )(core, *arrays)


def expert_sums(parts, unit_in, unit_out):
    rows = [x.shape[0] for x in parts]
    units = unit_in.shape[0]
    vmem = pl.BlockSpec(memory_space=pltpu.VMEM)
    return pl.pallas_call(
        functools.partial(expert_kernel, len(parts)),
        out_shape=[jax.ShapeDtypeStruct((r, D), jnp.bfloat16) for r in rows],
        in_specs=[vmem] * (len(parts) + 2),
        out_specs=[vmem] * len(parts),
        compiler_params=pltpu.CompilerParams(vmem_limit_bytes=EXPERT_VMEM),
        cost_estimate=pl.CostEstimate(flops=1, bytes_accessed=1, transcendentals=0),
        name="expert",
    )(*parts, unit_in, unit_out)


def local(kernel, outs, *args, name):
    vmem = pl.BlockSpec(memory_space=pltpu.VMEM)
    moved = sum(x.size * x.dtype.itemsize for x in (*args, *outs))
    return pl.pallas_call(
        kernel,
        out_shape=outs,
        in_specs=[vmem] * len(args),
        out_specs=[vmem] * len(outs),
        compiler_params=pltpu.CompilerParams(vmem_limit_bytes=EXPERT_VMEM),
        cost_estimate=pl.CostEstimate(
            flops=moved // 2, bytes_accessed=moved, transcendentals=0
        ),
        name=name,
    )(*args)


def rows_like(rows):
    return jax.ShapeDtypeStruct((rows, D), jnp.bfloat16)


def join_slots(stayed, crossed):
    capacity = stayed[0].shape[0]
    if capacity % 8:
        return [
            jnp.concatenate([rows, crossed[i * capacity : (i + 1) * capacity]], axis=0)
            for i, rows in enumerate(stayed)
        ]

    def kernel(*refs):
        count = len(stayed)
        other = refs[count][...].astype(jnp.float32)
        for i in range(count):
            pair = [refs[i][...].astype(jnp.float32), other[i * capacity : (i + 1) * capacity]]
            refs[count + 1 + i][...] = jnp.concatenate(pair, axis=0).astype(jnp.bfloat16)

    outs = [rows_like(2 * capacity) for _ in stayed]
    return local(kernel, outs, *stayed, crossed, name="join_slots")


def add_sums(parts, totals):
    def kernel(*refs):
        for part_ref, total_ref, out_ref in zip(refs[:2], refs[2:4], refs[4:]):
            total = part_ref[...].astype(jnp.float32) + total_ref[...].astype(jnp.float32)
            out_ref[...] = total.astype(jnp.bfloat16)

    return local(kernel, [rows_like(x.shape[0]) for x in parts], *parts, *totals, name="add_sums")


def finish_sums(*terms, pieces=1):
    size = terms[0].shape[0] // pieces

    def kernel(*refs):
        total = refs[0][...].astype(jnp.float32)
        for ref in refs[1 : len(terms)]:
            total = total + ref[...].astype(jnp.float32)
        for i, out_ref in enumerate(refs[len(terms) :]):
            out_ref[...] = total[i * size : (i + 1) * size].astype(jnp.bfloat16)

    return local(kernel, [rows_like(size)] * pieces, *terms, name="finish_sums")


def combine_kernel(blocks, state_ref, scale_ref, undo_ref, *refs):
    if refs[0].shape[0] % 8 == 0:
        rows = [ref[...].astype(jnp.float32) for ref in refs[:blocks]]
        rows = [jnp.concatenate(rows, axis=0).astype(jnp.bfloat16)]
    else:
        rows = [ref[...] for ref in refs[:blocks]]
    begin, total = 0, None
    for part in rows:
        pick = undo_ref[:, begin : begin + part.shape[0]]
        begin += part.shape[0]
        part = jnp.dot(pick, part, preferred_element_type=jnp.float32)
        total = part if total is None else total + part
    refs[blocks][...] = (state_ref[...] + scale_ref[...] * total).astype(jnp.bfloat16)


def combine(state, scale, undo, returned):
    tok_count = state.shape[0]
    blocks = len(returned)
    vmem = pl.BlockSpec(memory_space=pltpu.VMEM)
    return pl.pallas_call(
        functools.partial(combine_kernel, blocks),
        out_shape=jax.ShapeDtypeStruct((tok_count, D), jnp.bfloat16),
        in_specs=[vmem] * (3 + blocks),
        out_specs=vmem,
        compiler_params=pltpu.CompilerParams(vmem_limit_bytes=EXPERT_VMEM),
        cost_estimate=pl.CostEstimate(
            flops=2 * tok_count * tok_count * D, bytes_accessed=4_000_000, transcendentals=0
        ),
        name="combine",
    )(state, scale, undo, *returned)


def body(
    queries, dec_state, enc_kv, band_start, norm_gain, route_ids, keep, route_prob, w_in, w_out
):
    sections = lax.axis_size("section")
    seqs = lax.axis_size("seq")
    depth = lax.axis_size("expert")
    chips = sections // CORES
    assert chips == 2 and w_in.shape[0] == CORES
    s = lax.axis_index("section")
    q = lax.axis_index("seq")
    core = s % CORES

    def route(source_of):
        pairs = []
        for a in range(sections):
            for b in range(seqs):
                origin = source_of(b)
                if origin is not None:
                    pairs.append((((a - 1) % sections) * seqs + origin, a * seqs + b))
        return pairs

    frames = enc_kv.shape[2]
    block = enc_kv[:, 0]
    if seqs == 2:
        shards = [
            lax.ppermute(block, ("section", "seq"), route(lambda b: 1 - b)),
            lax.ppermute(block, ("section", "seq"), route(lambda b: b)),
        ]
        origins = [1 - q, q]
    else:
        shards = [
            lax.ppermute(block, ("section", "seq"), route(lambda b: b)),
            lax.ppermute(block, ("section", "seq"), route(lambda b: b - 1 if b > 0 else None)),
            lax.ppermute(
                block, ("section", "seq"), route(lambda b: b + 1 if b < seqs - 1 else None)
            ),
        ]
        origins = [q, q - 1, q + 1]
    rel = jnp.stack([band_start[0, 0] - origin * frames for origin in origins]).astype(jnp.int32)

    def core_pairs():
        return [(a, a ^ 1) for a in range(sections)]

    core_at = core.astype(jnp.int32)[None]
    share = w_in.shape[1]
    pair_units = staged(
        pick_kernel, core_at, [w_in, w_out], [rows_like(share)] * 2, 2, "pick_units"
    )
    rel, pair_units = lax.optimization_barrier((rel, pair_units))
    pair_units = [lax.ppermute(rows, "section", core_pairs()) for rows in pair_units]

    experts_of = route_ids[0, :, 0]
    tok_count = experts_of.shape[0]
    expert_count = seqs * CORES
    capacity = max(2, tok_count // expert_count)
    one_hot = (experts_of[:, None] == jnp.arange(expert_count, dtype=jnp.int32)[None, :]).astype(
        jnp.int32
    )
    slot_of = jnp.sum((jnp.cumsum(one_hot, axis=0) - one_hot) * one_hot, axis=1)
    kept = keep[0] == 1
    turns = [(dq, dc) for dq in range(seqs) for dc in range(CORES)]
    slots = jnp.arange(capacity, dtype=jnp.int32)
    dispatch, undo = [], []
    for dq, dc in turns:
        named = ((q + dq) % seqs) * CORES + (core ^ dc)
        code = jnp.where(kept & (experts_of == named), slot_of, -1)
        dispatch.append((slots[:, None] == code[None, :]).astype(jnp.bfloat16))
        undo.append((code[:, None] == slots[None, :]).astype(jnp.bfloat16))
    undo = jnp.concatenate(undo, axis=1)
    scale = (keep[0].astype(jnp.float32) * route_prob[0])[:, None]

    crossing = jnp.concatenate(
        [rows for (dq, dc), rows in zip(turns, dispatch) if dc == 1], axis=0
    )
    staying = [rows for (dq, dc), rows in zip(turns, dispatch) if dc == 0]
    ready, rel, crossing, staying, undo, scale = lax.optimization_barrier(
        (core_at, rel, crossing, staying, undo, scale)
    )
    query_rows, residual = staged(
        stage_kernel,
        ready,
        [queries[0], dec_state[0]],
        [rows_like(tok_count)] * 2,
        2,
        "stage_rows",
    )
    state, crossed, *stayed = attend(
        rel, query_rows, residual, norm_gain[None, :], shards, [crossing] + staying
    )

    def core_swap(rows):
        return lax.ppermute(rows, "section", core_pairs())

    def seq_move(rows, step):
        return lax.ppermute(rows, "seq", [(b, (b + step) % seqs) for b in range(seqs)])

    slot_blocks = join_slots(stayed, core_swap(crossed))
    moved = [seq_move(slot_blocks[dq], dq) for dq in range(1, seqs)]
    parts = [slot_blocks[0], moved[0] if seqs == 2 else jnp.concatenate(moved, axis=0)]

    unit_in, unit_out = staged(
        pool_kernel,
        core_at,
        [w_in, w_out, *pair_units],
        [rows_like(CORES * share)] * 2,
        4,
        "pool_units",
    )
    parts[1], unit_in, unit_out = lax.optimization_barrier((parts[1], unit_in, unit_out))

    cycle = [(0, z) for z in range(depth)] + [(1, z) for z in reversed(range(depth))]
    count = len(cycle)

    def hop(rows, step):
        pairs = []
        for c in range(CORES):
            ids = [(x * CORES + c) * depth + z for x, z in cycle]
            pairs += [(ids[i], ids[(i + step) % count]) for i in range(count)]
        return lax.ppermute(rows, ("section", "expert"), pairs)

    half = count // 2
    fore = [[rows] for rows in parts]
    rear = [[rows] for rows in parts]
    sums = {}

    def after(keys, rows):
        for key in keys:
            if key in sums:
                rows, sums[key] = lax.optimization_barrier((rows, sums[key]))
        return rows

    def sums_of(*rows):
        return expert_sums(list(rows), unit_in, unit_out)

    for k in range(1, half):
        for p in range(2):
            rows = (fore[p][-1], rear[p][-1])
            rows = lax.optimization_barrier(rows)
            if p == 1:
                rows = after([(0, k - 1), (1, k - 2)], rows)
            fore[p].append(hop(rows[0], 1))
            rear[p].append(hop(rows[1], -1))
            if k < half - 1:
                sums[p, k] = sums_of(fore[p][k], rear[p][k])
    fore[0].append(hop(fore[0][-1], 1))
    rear[1].append(hop(rear[1][-1], -1))
    ahead_part, behind_part = [{}, {}], [{}, {}]
    for (p, k), got in sums.items():
        behind_part[p][k], ahead_part[p][k] = got
    k = half - 1
    behind_part[0][k], ahead_part[1][k] = sums_of(fore[0][k], rear[1][k])
    ahead_part[0][k], behind_part[1][k] = sums_of(rear[0][k], fore[1][k])
    lead = [behind_part[0][k], ahead_part[1][k]]
    fore[0][half], lead = lax.optimization_barrier((fore[0][half], lead))
    behind_part[0][k], ahead_part[1][k] = lead
    ahead_part[0][half] = sums_of(fore[0][half])[0]
    behind_part[1][half] = sums_of(rear[1][half])[0]

    short = [hop(behind_part[0][half - 1], -1), hop(ahead_part[1][half - 1], 1)]
    long = [hop(ahead_part[0][half], 1), hop(behind_part[1][half], -1)]
    short, parts = lax.optimization_barrier((short, parts))
    own = sums_of(*parts)
    for k in range(half - 1, 0, -1):
        if k < half - 1:
            if k == 1:
                short, own = lax.optimization_barrier((short, own))
            totals = add_sums([behind_part[0][k], ahead_part[1][k]], short)
            short = [hop(totals[0], -1), hop(totals[1], 1)]
        if k > 1:
            totals = add_sums([ahead_part[0][k], behind_part[1][k]], long)
            long = [hop(totals[0], 1), hop(totals[1], -1)]
        else:
            far = hop(finish_sums(behind_part[1][k], long[1])[0], -1)
            near = hop(finish_sums(ahead_part[0][k], long[0])[0], 1)
            long = [near, far]

    def cross(rows, dq, dc):
        pairs = [
            ((a ^ dc) * seqs + (b + dq) % seqs, a * seqs + b)
            for a in range(sections)
            for b in range(seqs)
        ]
        return lax.ppermute(rows, ("section", "seq"), pairs)

    if seqs == 2 and capacity % 8 == 0:
        blocks = finish_sums(own[1], short[1], long[1], pieces=CORES)
        blocks = [*finish_sums(own[0], short[0], long[0], pieces=CORES), *blocks]
    else:
        near = finish_sums(own[0], short[0], long[0])[0]
        far = finish_sums(own[1], short[1], long[1])[0]
        blocks = [near[i * capacity : (i + 1) * capacity] for i in range(CORES)]
        blocks += [far[i * capacity : (i + 1) * capacity] for i in range(len(turns) - CORES)]
    returned = [
        cross(rows, dq, dc) if dq or dc else rows for (dq, dc), rows in zip(turns, blocks)
    ]
    return combine(state, scale, undo, returned)[None]


def solution(mesh):
    return jax.shard_map(
        body,
        mesh=mesh,
        in_specs=(
            P(("section", "expert"), "seq", None),
            P(("section", "expert"), "seq", None),
            P(None, ("section", "expert"), "seq", None),
            P(("section", "expert"), "seq"),
            P(),
            P(("section", "expert"), "seq", None),
            P(("section", "expert"), "seq"),
            P(("section", "expert"), "seq"),
            P("seq", ("section", "expert"), None),
            P("seq", ("section", "expert"), None),
        ),
        out_specs=P(("section", "expert"), "seq", None),
        check_vma=False,
    )
```

```python
import functools
import math

import jax
import jax.numpy as jnp
from jax import lax
from jax.experimental import pallas as pl
from jax.experimental.pallas import tpu as pltpu
from jax.sharding import PartitionSpec as P

D = 4096
HEADS = 32
KV_HEADS = 8
DH = 128
WIN = 128
CORES = 2
VMEM_LIMIT = 16 * 1024 * 1024
EXPERT_VMEM = 8 * 1024 * 1024
WIDE_VMEM = 56 * 1024 * 1024
SPAN = 1024


def attend_kernel(shards, blocks, rel_ref, q_ref, res_ref, gain_ref, *refs):
    kv_refs = refs[:shards]
    disp_refs = refs[shards : shards + blocks]
    state_ref = refs[shards + blocks]
    out_refs = refs[shards + blocks + 1 :]
    tok_count = q_ref.shape[0]
    groups = HEADS // KV_HEADS
    frames = kv_refs[0].shape[1]
    row = lax.broadcasted_iota(jnp.int32, (WIN, frames), 0)
    col = lax.broadcasted_iota(jnp.int32, (WIN, frames), 1)
    band = [None, None]
    for j in range(shards):
        pick = (col == row + rel_ref[j]).astype(jnp.bfloat16)
        for side in range(2):
            part = jnp.dot(pick, kv_refs[j][side], preferred_element_type=jnp.float32)
            band[side] = part if band[side] is None else band[side] + part
    keys_b = band[0].astype(jnp.bfloat16)
    values_b = band[1].astype(jnp.bfloat16)
    squares = jnp.zeros((tok_count, DH), jnp.float32)
    for g in range(KV_HEADS):
        key = keys_b[:, g * DH : (g + 1) * DH]
        value = values_b[:, g * DH : (g + 1) * DH]
        heads = [slice(h * DH, (h + 1) * DH) for h in range(g * groups, (g + 1) * groups)]
        grouped = jnp.concatenate([q_ref[:, cols] for cols in heads], axis=0)
        scores = lax.dot_general(
            grouped, key, (((1,), (1,)), ((), ())), preferred_element_type=jnp.float32
        ) * (1.0 / math.sqrt(DH))
        weights = jnp.exp(scores - jnp.max(scores, axis=-1, keepdims=True))
        total = jnp.sum(weights, axis=-1, keepdims=True)
        context = jnp.dot(
            weights.astype(jnp.bfloat16), value, preferred_element_type=jnp.float32
        ) / total
        for i, cols in enumerate(heads):
            state = res_ref[:, cols].astype(jnp.float32) + context[i * tok_count : (i + 1) * tok_count]
            state_ref[:, cols] = state
            squares = squares + state * state
    squares = jnp.sum(squares, axis=-1, keepdims=True)
    scale = lax.rsqrt(squares / D + 1e-06)
    normed = (state_ref[...] * scale * gain_ref[...]).astype(jnp.bfloat16)
    for disp_ref, out_ref in zip(disp_refs, out_refs):
        out_ref[...] = jnp.dot(
            disp_ref[...], normed, preferred_element_type=jnp.float32
        ).astype(jnp.bfloat16)


def attend(rel, query_rows, residual, gain, shards, dispatch):
    tok_count = query_rows.shape[0]
    vmem = pl.BlockSpec(memory_space=pltpu.VMEM)
    outs = [jax.ShapeDtypeStruct((tok_count, D), jnp.float32)]
    outs += [jax.ShapeDtypeStruct((d.shape[0], D), jnp.bfloat16) for d in dispatch]
    return pl.pallas_call(
        functools.partial(attend_kernel, len(shards), len(dispatch)),
        out_shape=outs,
        in_specs=[pl.BlockSpec(memory_space=pltpu.SMEM)]
        + [vmem] * (3 + len(shards) + len(dispatch)),
        out_specs=[vmem] * len(outs),
        compiler_params=pltpu.CompilerParams(vmem_limit_bytes=VMEM_LIMIT),
        cost_estimate=pl.CostEstimate(
            flops=6 * tok_count * D * WIN, bytes_accessed=6_000_000, transcendentals=HEADS * WIN * tok_count
        ),
        name="attend",
    )(rel, query_rows, residual, gain, *shards, *dispatch)


def expert_kernel(count, *refs):
    x_refs = refs[:count]
    in_ref, out_w_ref = refs[count], refs[count + 1]
    out_refs = refs[count + 2 :]
    joined = all(ref.shape[0] % 8 == 0 for ref in x_refs)
    groups = [x_refs] if joined else [[ref] for ref in x_refs]
    targets = [out_refs] if joined else [[ref] for ref in out_refs]
    for sources, outs in zip(groups, targets):
        if len(sources) == 1:
            rows_b = sources[0][...]
        elif all(ref.shape[0] % 16 == 0 for ref in sources):
            rows_b = jnp.concatenate([ref[...] for ref in sources], axis=0)
        else:
            rows_b = [ref[...].astype(jnp.float32) for ref in sources]
            rows_b = jnp.concatenate(rows_b, axis=0).astype(jnp.bfloat16)
        hidden = lax.dot_general(
            rows_b, in_ref[...], (((1,), (1,)), ((), ())), preferred_element_type=jnp.float32
        )
        hidden = jnp.maximum(hidden, 0.0).astype(jnp.bfloat16)
        for at in range(0, D, SPAN):
            cols = slice(at, at + SPAN)
            part = jnp.dot(hidden, out_w_ref[:, cols], preferred_element_type=jnp.float32)
            begin = 0
            for out_ref in outs:
                rows = part[begin : begin + out_ref.shape[0]]
                out_ref[:, cols] = rows.astype(jnp.bfloat16)
                begin += out_ref.shape[0]


def pick_kernel(core_ref, in_ref, out_w_ref, pair_in_ref, pair_out_ref, sems):
    other = 1 - core_ref[0]
    copies = [
        pltpu.make_async_copy(in_ref.at[other], pair_in_ref, sems.at[0]),
        pltpu.make_async_copy(out_w_ref.at[other], pair_out_ref, sems.at[1]),
    ]
    for copy in copies:
        copy.start()
    for copy in copies:
        copy.wait()


def stage_kernel(core_ref, q_ref, res_ref, q_out_ref, res_out_ref, sems):
    copies = [
        pltpu.make_async_copy(q_ref, q_out_ref, sems.at[0]),
        pltpu.make_async_copy(res_ref, res_out_ref, sems.at[1]),
    ]
    for copy in copies:
        copy.start()
    for copy in copies:
        copy.wait()


def pool_kernel(core_ref, in_ref, out_w_ref, pair_in_ref, pair_out_ref, unit_in_ref, unit_out_ref, sems):
    core = core_ref[0]
    units = pair_in_ref.shape[0]
    copies = []
    sources = [
        (in_ref.at[core], pair_in_ref, unit_in_ref),
        (out_w_ref.at[core], pair_out_ref, unit_out_ref),
    ]
    for mine, other, target in sources:
        for at, source in enumerate((mine, other)):
            copies.append(
                pltpu.make_async_copy(
                    source, target.at[pl.ds(at * units, units)], sems.at[len(copies)]
                )
            )
    for copy in copies:
        copy.start()
    for copy in copies:
        copy.wait()


def staged(kernel, core, arrays, outs, copies, name, limit=EXPERT_VMEM, space=pltpu.VMEM):
    target = pl.BlockSpec(memory_space=space)
    return pl.pallas_call(
        kernel,
        out_shape=outs,
        in_specs=[pl.BlockSpec(memory_space=pltpu.SMEM)]
        + [pl.BlockSpec(memory_space=pl.ANY)] * len(arrays),
        out_specs=[target] * len(outs),
        scratch_shapes=[pltpu.SemaphoreType.DMA((copies,))],
        compiler_params=pltpu.CompilerParams(vmem_limit_bytes=limit),
        cost_estimate=pl.CostEstimate(
            flops=0, bytes_accessed=sum(2 * x.size * 2 for x in outs), transcendentals=0
        ),
        name=name,
    )(core, *arrays)


def expert_sums(parts, unit_in, unit_out):
    rows = [x.shape[0] for x in parts]
    units = unit_in.shape[0]
    vmem = pl.BlockSpec(memory_space=pltpu.VMEM)
    return pl.pallas_call(
        functools.partial(expert_kernel, len(parts)),
        out_shape=[jax.ShapeDtypeStruct((r, D), jnp.bfloat16) for r in rows],
        in_specs=[vmem] * (len(parts) + 2),
        out_specs=[vmem] * len(parts),
        compiler_params=pltpu.CompilerParams(vmem_limit_bytes=EXPERT_VMEM),
        cost_estimate=pl.CostEstimate(flops=1, bytes_accessed=1, transcendentals=0),
        name="expert",
    )(*parts, unit_in, unit_out)


def local(kernel, outs, *args, name):
    vmem = pl.BlockSpec(memory_space=pltpu.VMEM)
    moved = sum(x.size * x.dtype.itemsize for x in (*args, *outs))
    return pl.pallas_call(
        kernel,
        out_shape=outs,
        in_specs=[vmem] * len(args),
        out_specs=[vmem] * len(outs),
        compiler_params=pltpu.CompilerParams(vmem_limit_bytes=EXPERT_VMEM),
        cost_estimate=pl.CostEstimate(
            flops=moved // 2, bytes_accessed=moved, transcendentals=0
        ),
        name=name,
    )(*args)


def rows_like(rows):
    return jax.ShapeDtypeStruct((rows, D), jnp.bfloat16)


def join_slots(stayed, crossed):
    capacity = stayed[0].shape[0]
    if capacity % 8:
        return [
            jnp.concatenate([rows, crossed[i * capacity : (i + 1) * capacity]], axis=0)
            for i, rows in enumerate(stayed)
        ]

    def kernel(*refs):
        count = len(stayed)
        other = refs[count][...].astype(jnp.float32)
        for i in range(count):
            pair = [refs[i][...].astype(jnp.float32), other[i * capacity : (i + 1) * capacity]]
            refs[count + 1 + i][...] = jnp.concatenate(pair, axis=0).astype(jnp.bfloat16)

    outs = [rows_like(2 * capacity) for _ in stayed]
    return local(kernel, outs, *stayed, crossed, name="join_slots")


def add_sums(parts, totals):
    def kernel(*refs):
        for part_ref, total_ref, out_ref in zip(refs[:2], refs[2:4], refs[4:]):
            total = part_ref[...].astype(jnp.float32) + total_ref[...].astype(jnp.float32)
            out_ref[...] = total.astype(jnp.bfloat16)

    return local(kernel, [rows_like(x.shape[0]) for x in parts], *parts, *totals, name="add_sums")


def finish_sums(*terms, pieces=1):
    size = terms[0].shape[0] // pieces

    def kernel(*refs):
        total = refs[0][...].astype(jnp.float32)
        for ref in refs[1 : len(terms)]:
            total = total + ref[...].astype(jnp.float32)
        for i, out_ref in enumerate(refs[len(terms) :]):
            out_ref[...] = total[i * size : (i + 1) * size].astype(jnp.bfloat16)

    return local(kernel, [rows_like(size)] * pieces, *terms, name="finish_sums")


def combine_kernel(blocks, state_ref, scale_ref, undo_ref, *refs):
    if refs[0].shape[0] % 8 == 0:
        rows = [ref[...].astype(jnp.float32) for ref in refs[:blocks]]
        rows = [jnp.concatenate(rows, axis=0).astype(jnp.bfloat16)]
    else:
        rows = [ref[...] for ref in refs[:blocks]]
    begin, total = 0, None
    for part in rows:
        pick = undo_ref[:, begin : begin + part.shape[0]]
        begin += part.shape[0]
        part = jnp.dot(pick, part, preferred_element_type=jnp.float32)
        total = part if total is None else total + part
    refs[blocks][...] = (state_ref[...] + scale_ref[...] * total).astype(jnp.bfloat16)


def combine(state, scale, undo, returned):
    tok_count = state.shape[0]
    blocks = len(returned)
    vmem = pl.BlockSpec(memory_space=pltpu.VMEM)
    return pl.pallas_call(
        functools.partial(combine_kernel, blocks),
        out_shape=jax.ShapeDtypeStruct((tok_count, D), jnp.bfloat16),
        in_specs=[vmem] * (3 + blocks),
        out_specs=vmem,
        compiler_params=pltpu.CompilerParams(vmem_limit_bytes=EXPERT_VMEM),
        cost_estimate=pl.CostEstimate(
            flops=2 * tok_count * tok_count * D, bytes_accessed=4_000_000, transcendentals=0
        ),
        name="combine",
    )(state, scale, undo, *returned)


def body(
    queries, dec_state, enc_kv, band_start, norm_gain, route_ids, keep, route_prob, w_in, w_out
):
    sections = lax.axis_size("section")
    seqs = lax.axis_size("seq")
    depth = lax.axis_size("expert")
    chips = sections // CORES
    assert chips == 2 and w_in.shape[0] == CORES
    s = lax.axis_index("section")
    q = lax.axis_index("seq")
    core = s % CORES

    def route(source_of):
        pairs = []
        for a in range(sections):
            for b in range(seqs):
                origin = source_of(b)
                if origin is not None:
                    pairs.append((((a - 1) % sections) * seqs + origin, a * seqs + b))
        return pairs

    frames = enc_kv.shape[2]
    block = enc_kv[:, 0]
    if seqs == 2:
        shards = [
            lax.ppermute(block, ("section", "seq"), route(lambda b: 1 - b)),
            lax.ppermute(block, ("section", "seq"), route(lambda b: b)),
        ]
        origins = [1 - q, q]
    else:
        shards = [
            lax.ppermute(block, ("section", "seq"), route(lambda b: b)),
            lax.ppermute(block, ("section", "seq"), route(lambda b: b - 1 if b > 0 else None)),
            lax.ppermute(
                block, ("section", "seq"), route(lambda b: b + 1 if b < seqs - 1 else None)
            ),
        ]
        origins = [q, q - 1, q + 1]
    rel = jnp.stack([band_start[0, 0] - origin * frames for origin in origins]).astype(jnp.int32)

    def core_pairs():
        return [(a, a ^ 1) for a in range(sections)]

    core_at = core.astype(jnp.int32)[None]
    share = w_in.shape[1]
    pair_units = staged(
        pick_kernel,
        core_at,
        [w_in, w_out],
        [rows_like(share)] * 2,
        2,
        "pick_units",
        limit=WIDE_VMEM,
    )
    rel, pair_units = lax.optimization_barrier((rel, pair_units))
    pair_units = [lax.ppermute(rows, "section", core_pairs()) for rows in pair_units]

    experts_of = route_ids[0, :, 0]
    tok_count = experts_of.shape[0]
    expert_count = seqs * CORES
    capacity = max(2, tok_count // expert_count)
    one_hot = (experts_of[:, None] == jnp.arange(expert_count, dtype=jnp.int32)[None, :]).astype(
        jnp.int32
    )
    slot_of = jnp.sum((jnp.cumsum(one_hot, axis=0) - one_hot) * one_hot, axis=1)
    kept = keep[0] == 1
    turns = [(dq, dc) for dq in range(seqs) for dc in range(CORES)]
    slots = jnp.arange(capacity, dtype=jnp.int32)
    dispatch, undo = [], []
    for dq, dc in turns:
        named = ((q + dq) % seqs) * CORES + (core ^ dc)
        code = jnp.where(kept & (experts_of == named), slot_of, -1)
        dispatch.append((slots[:, None] == code[None, :]).astype(jnp.bfloat16))
        undo.append((code[:, None] == slots[None, :]).astype(jnp.bfloat16))
    undo = jnp.concatenate(undo, axis=1)
    scale = (keep[0].astype(jnp.float32) * route_prob[0])[:, None]

    crossing = jnp.concatenate(
        [rows for (dq, dc), rows in zip(turns, dispatch) if dc == 1], axis=0
    )
    staying = [rows for (dq, dc), rows in zip(turns, dispatch) if dc == 0]
    ready, rel, crossing, staying, undo, scale = lax.optimization_barrier(
        (core_at, rel, crossing, staying, undo, scale)
    )
    query_rows, residual = staged(
        stage_kernel,
        ready,
        [queries[0], dec_state[0]],
        [rows_like(tok_count)] * 2,
        2,
        "stage_rows",
    )
    state, crossed, *stayed = attend(
        rel, query_rows, residual, norm_gain[None, :], shards, [crossing] + staying
    )

    def core_swap(rows):
        return lax.ppermute(rows, "section", core_pairs())

    def seq_move(rows, step):
        return lax.ppermute(rows, "seq", [(b, (b + step) % seqs) for b in range(seqs)])

    slot_blocks = join_slots(stayed, core_swap(crossed))
    moved = [seq_move(slot_blocks[dq], dq) for dq in range(1, seqs)]
    parts = [slot_blocks[0], moved[0] if seqs == 2 else jnp.concatenate(moved, axis=0)]

    unit_in, unit_out = staged(
        pool_kernel,
        core_at,
        [w_in, w_out, *pair_units],
        [rows_like(CORES * share)] * 2,
        4,
        "pool_units",
    )
    parts[1], unit_in, unit_out = lax.optimization_barrier((parts[1], unit_in, unit_out))

    cycle = [(0, z) for z in range(depth)] + [(1, z) for z in reversed(range(depth))]
    count = len(cycle)

    def hop(rows, step):
        pairs = []
        for c in range(CORES):
            ids = [(x * CORES + c) * depth + z for x, z in cycle]
            pairs += [(ids[i], ids[(i + step) % count]) for i in range(count)]
        return lax.ppermute(rows, ("section", "expert"), pairs)

    half = count // 2
    fore = [[rows] for rows in parts]
    rear = [[rows] for rows in parts]
    sums = {}

    def after(keys, rows):
        for key in keys:
            if key in sums:
                rows, sums[key] = lax.optimization_barrier((rows, sums[key]))
        return rows

    def sums_of(*rows):
        return expert_sums(list(rows), unit_in, unit_out)

    for k in range(1, half):
        for p in range(2):
            rows = (fore[p][-1], rear[p][-1])
            rows = lax.optimization_barrier(rows)
            if p == 1:
                rows = after([(0, k - 1), (1, k - 2)], rows)
            fore[p].append(hop(rows[0], 1))
            rear[p].append(hop(rows[1], -1))
            if k < half - 1:
                sums[p, k] = sums_of(fore[p][k], rear[p][k])
    fore[0].append(hop(fore[0][-1], 1))
    rear[1].append(hop(rear[1][-1], -1))
    ahead_part, behind_part = [{}, {}], [{}, {}]
    for (p, k), got in sums.items():
        behind_part[p][k], ahead_part[p][k] = got
    k = half - 1
    behind_part[0][k], ahead_part[1][k] = sums_of(fore[0][k], rear[1][k])
    ahead_part[0][k], behind_part[1][k] = sums_of(rear[0][k], fore[1][k])
    lead = [behind_part[0][k], ahead_part[1][k]]
    fore[0][half], lead = lax.optimization_barrier((fore[0][half], lead))
    behind_part[0][k], ahead_part[1][k] = lead
    ahead_part[0][half] = sums_of(fore[0][half])[0]
    behind_part[1][half] = sums_of(rear[1][half])[0]

    short = [hop(behind_part[0][half - 1], -1), hop(ahead_part[1][half - 1], 1)]
    long = [hop(ahead_part[0][half], 1), hop(behind_part[1][half], -1)]
    short, parts = lax.optimization_barrier((short, parts))
    own = sums_of(*parts)
    for k in range(half - 1, 0, -1):
        if k < half - 1:
            if k == 1:
                short, own = lax.optimization_barrier((short, own))
            totals = add_sums([behind_part[0][k], ahead_part[1][k]], short)
            short = [hop(totals[0], -1), hop(totals[1], 1)]
        if k > 1:
            totals = add_sums([ahead_part[0][k], behind_part[1][k]], long)
            long = [hop(totals[0], 1), hop(totals[1], -1)]
        else:
            far = hop(finish_sums(behind_part[1][k], long[1])[0], -1)
            near = hop(finish_sums(ahead_part[0][k], long[0])[0], 1)
            long = [near, far]

    def cross(rows, dq, dc):
        pairs = [
            ((a ^ dc) * seqs + (b + dq) % seqs, a * seqs + b)
            for a in range(sections)
            for b in range(seqs)
        ]
        return lax.ppermute(rows, ("section", "seq"), pairs)

    if seqs == 2 and capacity % 8 == 0:
        blocks = finish_sums(own[1], short[1], long[1], pieces=CORES)
        blocks = [*finish_sums(own[0], short[0], long[0], pieces=CORES), *blocks]
    else:
        near = finish_sums(own[0], short[0], long[0])[0]
        far = finish_sums(own[1], short[1], long[1])[0]
        blocks = [near[i * capacity : (i + 1) * capacity] for i in range(CORES)]
        blocks += [far[i * capacity : (i + 1) * capacity] for i in range(len(turns) - CORES)]
    returned = [
        cross(rows, dq, dc) if dq or dc else rows for (dq, dc), rows in zip(turns, blocks)
    ]
    return combine(state, scale, undo, returned)[None]


def solution(mesh):
    return jax.shard_map(
        body,
        mesh=mesh,
        in_specs=(
            P(("section", "expert"), "seq", None),
            P(("section", "expert"), "seq", None),
            P(None, ("section", "expert"), "seq", None),
            P(("section", "expert"), "seq"),
            P(),
            P(("section", "expert"), "seq", None),
            P(("section", "expert"), "seq"),
            P(("section", "expert"), "seq"),
            P("seq", ("section", "expert"), None),
            P("seq", ("section", "expert"), None),
        ),
        out_specs=P(("section", "expert"), "seq", None),
        check_vma=False,
    )
```
